256 devices in a mesh: attn: 32 (over z, x), tp: 8 (over y, core).
Axes of the slice: x: 4, y: 4, z: 8, core: 2. Of those that a mesh axis runs over, the one named last changes fastest.
Arguments:
- hidden: bfloat16 [32, 2, 8192], P(None, None, 'attn'), may hold values from -40 to 40
- lengths: int32 [32], replicated, may hold values from 2048 to 4096, as said below
- slot_of: int32 [32], replicated, may hold values from 0 to 63, as said below
- kv_cache: bfloat16 [64, 2, 4096, 1024], P('attn', None, None, 'tp'), may hold values from -300 to 300
- attn_gain: float32 [8192], P('attn'), may hold values from 0.1 to 1.9
- w_query: bfloat16 [8192, 8192], P('attn', 'tp'), may hold values from -0.06629126 to 0.06629126
- key_matrix: bfloat16 [8192, 1024], P('attn', 'tp'), may hold values from -0.22097087 to 0.22097087
- value_matrix: bfloat16 [8192, 1024], P('attn', 'tp'), may hold values from -0.0625 to 0.0625
- w_attn_out: bfloat16 [8192, 8192], P('tp', 'attn'), may hold values from -0.1875 to 0.1875
- mamba_gain: float32 [8192], P('attn'), may hold values from 0.1 to 1.9
- w_mamba_in: bfloat16 [8192, 8, 4608], P('attn', 'tp'), may hold values from -0.0625 to 0.0625
- w_mamba_dt: bfloat16 [8192, 256], P('attn', 'tp'), may hold values from -0.0625 to 0.0625
- w_mamba_out: bfloat16 [16384, 8192], P('tp', 'attn'), may hold values from -0.046875 to 0.046875
- conv_weight: float32 [4, 8, 2560], P(None, 'tp'), may hold values from -3 to 3
- conv_bias: float32 [8, 2560], P('tp'), may hold values from -0.5 to 0.5
- conv_state: float32 [32, 3, 8, 2560], P('attn', None, 'tp'), may hold values from -6 to 6
- ssm_state: float32 [32, 256, 64, 256], P('attn', 'tp'), may hold values from -6 to 6
- a_log: float32 [256], P('tp'), may hold values from -3.9 to 0.7
- dt_bias: float32 [256], P('tp'), may hold values from -2 to 1
- skip_gain: float32 [256], P('tp'), may hold values from 0.25 to 12
- group_gain: float32 [8, 2048], P('tp'), may hold values from 0.1 to 1.9
- mlp_gain: float32 [8192], P('attn'), may hold values from 0.1 to 1.9
- w_up: bfloat16 [8192, 16384], P('attn', 'tp'), may hold values from -0.0625 to 0.0625
- w_down: bfloat16 [16384, 8192], P('tp', 'attn'), may hold values from -0.046875 to 0.046875
Outputs:
- result: bfloat16 [32, 2, 8192], P(None, None, 'attn')
The draws below stay inside these ranges and needn't reach their ends.
Inputs may be any that keep to these rules, and one draw needn't show every extreme that they name: `lengths`: cache positions below a request's length hold its earlier tokens; some request has exactly 4096. Request r is in slot slot_of[r] of kv_cache, held by attention device slot_of[r] // 2; no two requests share a slot; some device holds 2 requests, some none.
All inputs are finite; a program needn't handle non-finite values.
Results may differ from the reference program's by a relative error of at most 0.027.
Values may be sent and summed in bfloat16 or wider, within the bound.
No kernel may reach another device: no remote copies, remote signals or barrier semaphores. Data moves between devices by JAX's collectives and lax.ppermute only.
A program may use at most 64 MiB of HBM per device.

```python
import math
import jax
import jax.numpy as jnp
from jax import lax

MODEL_WIDTH = 8192
HQ = 64
KEY_VALUE_HEADS = 8
HEAD_SIZE = 128
MH = 256
MP = 64
NS = 256
NG = 8
KC = 4
FW = 16384
STEPS = 2
DEVICE_SLOTS = 2
SLOT_POSITIONS = 4096
REQ = 32
SLOT_TOTAL = 64
GW = 4608
CW = 2560


def shared_key_columns(key):
    columns = jnp.clip(jax.random.normal(jax.random.fold_in(key, 21), (MODEL_WIDTH, KEY_VALUE_HEADS, HEAD_SIZE), jnp.float32), -4.0, 4.0) * MODEL_WIDTH ** (-0.5)
    head_rates = jnp.exp(jax.random.uniform(jax.random.fold_in(key, 22), (KEY_VALUE_HEADS,), jnp.float32, math.log(0.5), math.log(1.6)))
    head_rates = head_rates * (math.log(SLOT_POSITIONS) + 2.0) / math.sqrt(0.5 * HEAD_SIZE)
    return (columns, head_rates)


def draw_hidden(key, part):
    key = jax.random.fold_in(key, 11)
    key_column, key_row, key_base = jax.random.split(key, 3)
    column = jnp.arange(MODEL_WIDTH, dtype=jnp.float32) / MODEL_WIDTH
    column_scale = jnp.sqrt(1.0 + 2.0 * column) * jnp.exp(jax.random.uniform(key_column, (MODEL_WIDTH,), jnp.float32, 0.0, math.log(3.2)))
    row_scales = jnp.exp(jax.random.uniform(key_row, (REQ, STEPS, 1), jnp.float32, 0.0, math.log(3.2)))
    base = jnp.clip(jax.random.normal(key_base, (REQ, STEPS, MODEL_WIDTH), jnp.float32), -5.0, 5.0)
    return (base * row_scales * column_scale / 2.5).astype(jnp.bfloat16)


def draw_lengths(key, part):
    key = jax.random.fold_in(key, 12)
    key_length, key_pick = jax.random.split(key, 2)
    drawn = jax.random.randint(key_length, (REQ,), SLOT_POSITIONS // 2, SLOT_POSITIONS + 1, dtype=jnp.int32)
    chosen = jax.random.randint(key_pick, (), 0, REQ, dtype=jnp.int32)
    return jnp.where(jnp.arange(REQ, dtype=jnp.int32) == chosen, SLOT_POSITIONS, drawn).astype(jnp.int32)


def draw_slot_of(key, part):
    key = jax.random.fold_in(key, 13)
    score_key, device_key, key_order = jax.random.split(key, 3)
    slot_numbers = jnp.arange(SLOT_TOTAL, dtype=jnp.int32)
    score_values = jax.random.randint(score_key, (SLOT_TOTAL,), 0, 2 ** 20, dtype=jnp.int32) * SLOT_TOTAL + slot_numbers
    device_number = jax.random.randint(device_key, (), 0, SLOT_TOTAL // DEVICE_SLOTS, dtype=jnp.int32)
    forced_choice = (slot_numbers // DEVICE_SLOTS == device_number) | (slot_numbers == 0) | (slot_numbers == SLOT_TOTAL - 1)
    score_values = jnp.where(forced_choice, slot_numbers - SLOT_TOTAL, score_values)
    chosen = jnp.argsort(score_values, stable=True)[:REQ].astype(jnp.int32)
    order = jax.random.permutation(key_order, REQ)
    return chosen[order].astype(jnp.int32)


def draw_kv_cache(key, part):
    key = jax.random.fold_in(key, 14)
    key_base = jax.random.fold_in(key, 0)
    layer_width = KEY_VALUE_HEADS * HEAD_SIZE
    array_shape = (SLOT_TOTAL, 2, SLOT_POSITIONS, layer_width)
    spread = jnp.array([2.0, 1.0], jnp.float32).reshape(1, 2, 1, 1)
    base = jnp.clip(jax.random.normal(key_base, array_shape, jnp.float32), -6.0, 6.0) * spread
    return base.astype(jnp.bfloat16)


def draw_w_query(key, part):
    columns, head_rates = shared_key_columns(key)
    key = jax.random.fold_in(key, 15)
    per_key = HQ // KEY_VALUE_HEADS
    noise = jnp.clip(jax.random.normal(key, (MODEL_WIDTH, KEY_VALUE_HEADS, per_key, HEAD_SIZE), jnp.float32), -4.0, 4.0) * MODEL_WIDTH ** (-0.5)
    weight = math.sqrt(0.5) * (columns[:, :, None, :] + noise)
    return weight.reshape(MODEL_WIDTH, HQ * HEAD_SIZE).astype(jnp.bfloat16)


def draw_key_matrix(key, part):
    columns, head_rates = shared_key_columns(key)
    key = jax.random.fold_in(key, 16)
    noise = jnp.clip(jax.random.normal(key, (MODEL_WIDTH, KEY_VALUE_HEADS, HEAD_SIZE), jnp.float32), -4.0, 4.0) * MODEL_WIDTH ** (-0.5)
    weight = head_rates[None, :, None] * (columns + 0.3 * noise)
    return weight.reshape(MODEL_WIDTH, KEY_VALUE_HEADS * HEAD_SIZE).astype(jnp.bfloat16)


def block_levels(rng, dims, cuts, low, largest):
    level, own = 1.0, jax.random.fold_in(rng, 6)
    for dim, blocks in cuts:
        draws = jnp.exp(jax.random.uniform(jax.random.fold_in(own, dim), (blocks,), jnp.float32, low / len(cuts), largest / len(cuts)))
        level = level * jnp.repeat(draws, dims[dim] // blocks).reshape([-1 if axis == dim else 1 for axis in range(len(dims))])
    return level


def normal_values(stream_key, dims, scale, reach, shards=(), kind=jnp.bfloat16):
    values = jax.random.normal(stream_key, dims, jnp.float32) * scale
    if len(shards) > 0:
        values = block_levels(stream_key, dims, shards, -0.22, 0.18) * values
    return jnp.clip(values, min=-reach, max=reach).astype(kind)


def setup_inputs(seed: int = 0) -> dict:
    key_of = jax.random.split(jax.random.key(seed), 25)
    return {
        "hidden": draw_hidden(jax.random.fold_in(key_of[24], 71), 0),
        "lengths": draw_lengths(jax.random.fold_in(key_of[24], 71), 0),
        "slot_of": draw_slot_of(jax.random.fold_in(key_of[24], 71), 0),
        "kv_cache": draw_kv_cache(jax.random.fold_in(key_of[24], 71), 0),
        "attn_gain": jnp.clip(1.0 + 0.18 * jax.random.normal(key_of[4], (MODEL_WIDTH,), jnp.float32), 0.1, 1.9),
        "w_query": draw_w_query(jax.random.fold_in(key_of[24], 71), 0),
        "key_matrix": draw_key_matrix(jax.random.fold_in(key_of[24], 71), 0),
        "value_matrix": normal_values(key_of[7], (MODEL_WIDTH, KEY_VALUE_HEADS * HEAD_SIZE), MODEL_WIDTH ** -0.5, 0.0625, ((0, 32), (1, 8))),
        "w_attn_out": normal_values(key_of[8], (HQ * HEAD_SIZE, MODEL_WIDTH), (8 * HEAD_SIZE) ** -0.5, 0.1875, ((0, 8), (1, 32))),
        "mamba_gain": jnp.clip(1.0 + 0.18 * jax.random.normal(key_of[9], (MODEL_WIDTH,), jnp.float32), 0.1, 1.9),
        "w_mamba_in": normal_values(key_of[10], (MODEL_WIDTH, NG, GW), MODEL_WIDTH ** -0.5, 0.0625, ((0, 32), (1, 8))),
        "w_mamba_dt": normal_values(key_of[11], (MODEL_WIDTH, MH), MODEL_WIDTH ** -0.5, 0.0625, ((0, 32), (1, 8))),
        "w_mamba_out": normal_values(key_of[12], (MH * MP, MODEL_WIDTH), (MH * MP) ** -0.5, 0.046875, ((0, 8), (1, 32))),
        "conv_weight": normal_values(key_of[13], (KC, NG, CW), KC ** -0.5, 3.0, ((1, 8),), jnp.float32),
        "conv_bias": jnp.clip(jax.random.uniform(key_of[14], (NG, CW), jnp.float32, -0.5, 0.5) * block_levels(key_of[14], (NG, CW), ((0, 8),), -0.4, 0.0), -0.5, 0.5),
        "conv_state": normal_values(key_of[15], (REQ, KC - 1, NG, CW), 1.0, 6.0, ((0, 32), (2, 8)), jnp.float32),
        "ssm_state": normal_values(key_of[16], (REQ, MH, MP, NS), 1.0, 6.0, ((0, 32), (1, 8)), jnp.float32),
        "a_log": jnp.clip(-3.9 + 4.6 * jax.random.uniform(key_of[17], (MH,), jnp.float32) ** block_levels(key_of[17], (MH,), ((0, 8),), -0.2, 0.2), -3.9, 0.7),
        "dt_bias": jnp.clip(-2.0 + 3.0 * jax.random.uniform(key_of[18], (MH,), jnp.float32) ** block_levels(key_of[18], (MH,), ((0, 8),), -0.2, 0.2), -2.0, 1.0),
        "skip_gain": jnp.clip(jnp.exp(math.log(12.0) - 3.871201 * jax.random.uniform(key_of[19], (MH,), jnp.float32) ** block_levels(key_of[19], (MH,), ((0, 8),), -0.2, 0.2)), 0.25, 12.0),
        "group_gain": jnp.clip(1.0 + 0.18 * jax.random.normal(key_of[20], (NG, (MH // NG) * MP), jnp.float32), 0.1, 1.9),
        "mlp_gain": jnp.clip(1.0 + 0.18 * jax.random.normal(key_of[21], (MODEL_WIDTH,), jnp.float32), 0.1, 1.9),
        "w_up": normal_values(key_of[22], (MODEL_WIDTH, FW), MODEL_WIDTH ** -0.5, 0.0625, ((0, 32), (1, 8))),
        "w_down": normal_values(key_of[23], (FW, MODEL_WIDTH), FW ** -0.5, 0.046875, ((0, 8), (1, 32))),
    }


EPS = 1e-05
MASKED = -1e+30

def row_scale(values):
    widened = values.astype(jnp.float32)
    return lax.rsqrt(lax.optimization_barrier(jnp.mean(widened * widened, axis=-1)) + EPS)

def gained(values, gain):
    return (values.astype(jnp.float32) * gain).astype(jnp.bfloat16)

def project(normed, weight, scale):
    leading = normed.shape[:-1]
    flat_rows = normed.reshape(-1, normed.shape[-1])
    product = jnp.dot(flat_rows, weight.reshape(weight.shape[0], -1), preferred_element_type=jnp.float32)
    return product.reshape(leading + (-1,)) * scale[..., None]

def rounded(values):
    return lax.optimization_barrier(values.astype(jnp.bfloat16)).astype(jnp.float32)

def attend(query, new_keys, new_values, cache, length):
    steps = query.shape[0]
    kv_local = new_keys.shape[1] // HEAD_SIZE
    group = query.shape[1] // new_keys.shape[1]
    capacity = cache.shape[1]
    queries = query.astype(jnp.float32).reshape(steps, kv_local, group, HEAD_SIZE)
    old_keys = cache[0].astype(jnp.float32).reshape(capacity, kv_local, HEAD_SIZE)
    old_values = cache[1].astype(jnp.float32).reshape(capacity, kv_local, HEAD_SIZE)
    fresh_keys = new_keys.astype(jnp.float32).reshape(steps, kv_local, HEAD_SIZE)
    fresh_values = new_values.astype(jnp.float32).reshape(steps, kv_local, HEAD_SIZE)
    factor = HEAD_SIZE ** (-0.5)
    old_scores = jnp.einsum('sngd,cnd->sngc', queries, old_keys) * factor
    positions = jnp.arange(capacity, dtype=jnp.int32)
    old_scores = jnp.where(positions < length, old_scores, MASKED)
    fresh_scores = jnp.einsum('sngd,tnd->sngt', queries, fresh_keys) * factor
    later = jnp.arange(steps)[:, None] >= jnp.arange(steps)[None, :]
    fresh_scores = jnp.where(later[:, None, None, :], fresh_scores, MASKED)
    highest = jnp.maximum(old_scores.max(axis=-1), fresh_scores.max(axis=-1))
    old_weights = jnp.exp(old_scores - highest[..., None])
    fresh_weights = jnp.exp(fresh_scores - highest[..., None])
    total = old_weights.sum(axis=-1) + fresh_weights.sum(axis=-1)
    mixed = jnp.einsum('sngc,cnd->sngd', rounded(old_weights), old_values)
    mixed = mixed + jnp.einsum('sngt,tnd->sngd', rounded(fresh_weights), fresh_values)
    return (mixed / total[..., None]).reshape(steps, -1).astype(jnp.bfloat16)

def mamba_core(main_part, dt_raw, conv_prev, state, conv_weight, conv_bias, a_log, dt_bias, skip_gain, group_gain):
    steps, groups, _ = main_part.shape
    inner = group_gain.shape[1]
    heads = a_log.shape[0]
    per_group = heads // groups
    head_dim = inner // per_group
    states = state.shape[-1]
    state = state.reshape(groups, per_group, head_dim, states)
    gate = main_part[:, :, :inner]
    conv_in = main_part[:, :, inner:]
    window = jnp.concatenate([conv_prev, conv_in], axis=0)
    taps = conv_weight.shape[0]
    rates = jnp.exp(a_log).reshape(groups, per_group)
    step_size = jax.nn.softplus(dt_raw + dt_bias)
    skips = skip_gain.reshape(groups, per_group)
    outputs = []
    for position in range(steps):
        summed = conv_bias
        for tap_index in range(taps):
            summed = summed + conv_weight[tap_index] * window[position + tap_index]
        conved = jax.nn.silu(summed)
        inputs_x = conved[:, :inner].reshape(groups, per_group, head_dim)
        b_in = conved[:, inner:inner + states]
        c_out = conved[:, inner + states:]
        delta = step_size[position].reshape(groups, per_group)
        decay = jnp.exp(-delta * rates)
        state = state * decay[:, :, None, None] + (delta[:, :, None] * inputs_x)[..., None] * b_in[:, None, None, :]
        readout = lax.optimization_barrier(jnp.sum(state * c_out[:, None, None, :], axis=-1)) + skips[:, :, None] * inputs_x
        gated = readout.reshape(groups, inner) * jax.nn.silu(gate[position])
        normed = gated * lax.rsqrt(lax.optimization_barrier(jnp.mean(gated * gated, axis=-1, keepdims=True)) + EPS) * group_gain
        outputs.append(normed.reshape(-1))
    return jnp.stack(outputs).astype(jnp.bfloat16)

def reference(hidden, lengths, slot_of, kv_cache, attn_gain, w_query, key_matrix, value_matrix, w_attn_out, mamba_gain, w_mamba_in, w_mamba_dt, w_mamba_out, conv_weight, conv_bias, conv_state, ssm_state, a_log, dt_bias, skip_gain, group_gain, mlp_gain, w_up, w_down):
    requests, steps, layer_width = hidden.shape
    scale_attn = row_scale(hidden)
    normed_attn = gained(hidden, attn_gain)
    query = project(normed_attn, w_query, scale_attn).astype(jnp.bfloat16)
    new_keys = project(normed_attn, key_matrix, scale_attn).astype(jnp.bfloat16)
    new_values = project(normed_attn, value_matrix, scale_attn).astype(jnp.bfloat16)

    def per_request(inputs):
        one_query, one_key, one_value, slot, length = inputs
        cache = lax.dynamic_index_in_dim(kv_cache, slot.astype(jnp.int32), 0, keepdims=False)
        return attend(one_query, one_key, one_value, cache, length)
    heads_out = lax.map(per_request, (query, new_keys, new_values, slot_of, lengths))
    attn_out = jnp.dot(heads_out.reshape(requests * steps, -1), w_attn_out, preferred_element_type=jnp.float32)
    first = (hidden.astype(jnp.float32) + attn_out.reshape(requests, steps, layer_width)).astype(jnp.bfloat16)
    scale_mix = row_scale(first)
    normed_mix = gained(first, mamba_gain)
    main_part = project(normed_mix, w_mamba_in, scale_mix).reshape(requests, steps, NG, -1)
    dt_raw = project(normed_mix, w_mamba_dt, scale_mix)

    def per_mixer(inputs):
        one_main, one_dt, one_conv, one_state = inputs
        return mamba_core(one_main, one_dt, one_conv, one_state, conv_weight, conv_bias, a_log, dt_bias, skip_gain, group_gain)
    mixer = lax.map(per_mixer, (main_part, dt_raw, conv_state, ssm_state))
    mixed_out = jnp.dot(mixer.reshape(requests * steps, -1), w_mamba_out, preferred_element_type=jnp.float32)
    second = (first.astype(jnp.float32) + mixed_out.reshape(requests, steps, layer_width)).astype(jnp.bfloat16)
    scale_ff = row_scale(second)
    normed_ff = gained(second, mlp_gain)
    upward = jnp.maximum(project(normed_ff, w_up, scale_ff), 0.0)
    active = (upward * upward).astype(jnp.bfloat16)
    downward = jnp.dot(active.reshape(requests * steps, -1), w_down, preferred_element_type=jnp.float32)
    return (second.astype(jnp.float32) + downward.reshape(requests, steps, layer_width)).astype(jnp.bfloat16)
```

```python
import jax
import jax.numpy as jnp
from jax import lax
from jax.sharding import PartitionSpec as P

HEAD_SIZE = 128


EPS = 1e-05
MASKED = -1e30
SQUARE_COLUMNS = 128


def local_squares(values):
    widened = values.astype(jnp.float32)
    return jnp.sum(widened * widened, axis=-1)


def scale_from(squares, layer_width):
    return lax.rsqrt(squares / layer_width + EPS)


def gained(values, gain):
    return (values.astype(jnp.float32) * gain).astype(jnp.bfloat16)


def hi_lo(squares):
    high = squares.astype(jnp.bfloat16)
    low = (squares - high.astype(jnp.float32)).astype(jnp.bfloat16)
    pair = jnp.stack([high, low], axis=-1)
    return jnp.pad(pair, [(0, 0)] * (pair.ndim - 1) + [(0, SQUARE_COLUMNS - 2)])


def spread(values, axis):
    copies = jnp.broadcast_to(values[None], (lax.axis_size(axis),) + values.shape)
    return lax.all_to_all(copies, axis, 0, 0)


def gather_sum(values, axis):
    return jnp.sum(lax.all_to_all(values, axis, 0, 0).astype(jnp.float32), axis=0)


def tp_sum(values):
    return jnp.sum(spread(values.astype(jnp.bfloat16), "tp").astype(jnp.float32), axis=0)


def attend(query, new_keys, new_values, cache, length):
    steps = query.shape[0]
    kv_local = new_keys.shape[1] // HEAD_SIZE
    group = query.shape[1] // new_keys.shape[1]
    capacity = cache.shape[1]
    queries = query.reshape(steps, kv_local, group, HEAD_SIZE)
    old_keys = cache[0].reshape(capacity, kv_local, HEAD_SIZE)
    old_values = cache[1].reshape(capacity, kv_local, HEAD_SIZE)
    fresh_keys = new_keys.reshape(steps, kv_local, HEAD_SIZE)
    fresh_values = new_values.reshape(steps, kv_local, HEAD_SIZE)
    factor = HEAD_SIZE ** (-0.5)
    old_scores = (
        jnp.einsum("sngd,cnd->sngc", queries, old_keys, preferred_element_type=jnp.float32) * factor
    )
    positions = jnp.arange(capacity, dtype=jnp.int32)
    old_scores = jnp.where(positions < length, old_scores, MASKED)
    fresh_scores = (
        jnp.einsum("sngd,tnd->sngt", queries, fresh_keys, preferred_element_type=jnp.float32)
        * factor
    )
    later = jnp.arange(steps)[:, None] >= jnp.arange(steps)[None, :]
    fresh_scores = jnp.where(later[:, None, None, :], fresh_scores, MASKED)
    highest = jnp.maximum(old_scores.max(axis=-1), fresh_scores.max(axis=-1))
    old_weights = jnp.exp(old_scores - highest[..., None])
    fresh_weights = jnp.exp(fresh_scores - highest[..., None])
    total = old_weights.sum(axis=-1) + fresh_weights.sum(axis=-1)
    mixed = jnp.einsum(
        "sngc,cnd->sngd",
        old_weights.astype(jnp.bfloat16),
        old_values,
        preferred_element_type=jnp.float32,
    )
    mixed = mixed + jnp.einsum(
        "sngt,tnd->sngd",
        fresh_weights.astype(jnp.bfloat16),
        fresh_values,
        preferred_element_type=jnp.float32,
    )
    return (mixed / total[..., None]).reshape(steps, -1).astype(jnp.bfloat16)


def mamba_core(
    main_part,
    dt_raw,
    conv_prev,
    state,
    conv_weight,
    conv_bias,
    a_log,
    dt_bias,
    skip_gain,
    group_gain,
):
    steps, groups, _ = main_part.shape
    inner = group_gain.shape[1]
    heads = a_log.shape[0]
    per_group = heads // groups
    head_dim = inner // per_group
    states = state.shape[-1]
    state = state.reshape(groups, per_group, head_dim, states)
    gate = main_part[:, :, :inner]
    conv_in = main_part[:, :, inner:]
    window = jnp.concatenate([conv_prev, conv_in], axis=0)
    taps = conv_weight.shape[0]
    rates = jnp.exp(a_log).reshape(groups, per_group)
    step_size = jax.nn.softplus(dt_raw + dt_bias)
    skips = skip_gain.reshape(groups, per_group)
    outputs = []
    for position in range(steps):
        summed = conv_bias
        for tap_index in range(taps):
            summed = summed + conv_weight[tap_index] * window[position + tap_index]
        conved = jax.nn.silu(summed)
        inputs_x = conved[:, :inner].reshape(groups, per_group, head_dim)
        b_in = conved[:, inner : inner + states]
        c_out = conved[:, inner + states :]
        delta = step_size[position].reshape(groups, per_group)
        decay = jnp.exp(-delta * rates)
        state = (
            state * decay[:, :, None, None]
            + (delta[:, :, None] * inputs_x)[..., None] * b_in[:, None, None, :]
        )
        readout = jnp.sum(state * c_out[:, None, None, :], axis=-1) + skips[:, :, None] * inputs_x
        gated = readout.reshape(groups, inner) * jax.nn.silu(gate[position])
        normed = (
            gated * lax.rsqrt(jnp.mean(gated * gated, axis=-1, keepdims=True) + EPS) * group_gain
        )
        outputs.append(normed.reshape(-1))
    return jnp.stack(outputs).astype(jnp.bfloat16)


def squared_relu(values):
    lifted = jnp.maximum(values, 0.0)
    return (lifted * lifted).astype(jnp.bfloat16)


def on_device(
    hidden,
    lengths,
    slot_of,
    kv_cache,
    attn_gain,
    w_query,
    key_matrix,
    value_matrix,
    w_attn_out,
    mamba_gain,
    w_mamba_in,
    w_mamba_dt,
    w_mamba_out,
    conv_weight,
    conv_bias,
    conv_state,
    ssm_state,
    a_log,
    dt_bias,
    skip_gain,
    group_gain,
    mlp_gain,
    w_up,
    w_down,
):
    requests, steps, local_width = hidden.shape
    devices = lax.axis_size("attn")
    layer_width = local_width * devices
    slots = kv_cache.shape[0]
    total_slots = slots * devices
    position_here = lax.axis_index("attn")
    slot_numbers = jnp.arange(total_slots, dtype=jnp.int32)
    placed = slot_numbers[:, None] == slot_of[None, :]
    own_slots = lax.dynamic_slice_in_dim(placed, position_here * slots, slots, 0)
    slot_length = jnp.sum(jnp.where(own_slots, lengths[None, :], 0), axis=1)
    query_cols = w_query.shape[1]
    key_cols = key_matrix.shape[1]
    squares_attn = local_squares(hidden)
    normed_attn = gained(hidden, attn_gain)
    flat_rows = normed_attn.reshape(requests * steps, local_width)
    by_slot = jnp.einsum(
        "jr,rsd->jsd", placed.astype(jnp.bfloat16), normed_attn,
        preferred_element_type=jnp.float32,
    ).astype(jnp.bfloat16).reshape(total_slots * steps, local_width)
    squares_by_slot = jnp.einsum(
        "jr,rs->js", placed.astype(jnp.float32), squares_attn, precision=lax.Precision.HIGHEST
    ).reshape(total_slots * steps)
    weights_in = jnp.concatenate([w_query, key_matrix, value_matrix], axis=1)
    parts = jnp.dot(by_slot, weights_in, preferred_element_type=jnp.float32).astype(jnp.bfloat16)
    parts = jnp.concatenate([parts, hi_lo(squares_by_slot)], axis=1)
    summed = gather_sum(parts.reshape(devices, slots * steps, -1), "attn")
    all_cols = query_cols + 2 * key_cols
    scale_attn = scale_from(summed[:, all_cols] + summed[:, all_cols + 1], layer_width)
    projected = (summed[:, :all_cols] * scale_attn[:, None]).astype(jnp.bfloat16)
    projected = projected.reshape(slots, steps, all_cols)
    query = projected[..., :query_cols]
    new_keys = projected[..., query_cols : query_cols + key_cols]
    new_values = projected[..., query_cols + key_cols :]
    slot_outputs = jax.vmap(attend)(query, new_keys, new_values, kv_cache, slot_length)
    every_slot = spread(slot_outputs.reshape(slots * steps, -1), "attn")
    by_request = jnp.einsum(
        "jr,jsd->rsd",
        placed.astype(jnp.bfloat16),
        every_slot.reshape(total_slots, steps, -1),
        preferred_element_type=jnp.float32,
    ).astype(jnp.bfloat16)
    request_result = jnp.dot(
        by_request.reshape(requests * steps, -1), w_attn_out, preferred_element_type=jnp.float32
    ).reshape(requests, steps, local_width)
    first = (hidden.astype(jnp.float32) + tp_sum(request_result)).astype(jnp.bfloat16)
    squares_mix = local_squares(first)
    normed_mix = gained(first, mamba_gain)
    groups_local = w_mamba_in.shape[1]
    main_cols = groups_local * w_mamba_in.shape[2]
    mix_cols = main_cols + w_mamba_dt.shape[1]
    w_main = w_mamba_in.reshape(local_width, main_cols)
    own_rows = conv_state.shape[0]
    block = normed_mix.reshape(requests * steps, local_width)
    main_term = jnp.dot(block, w_main, preferred_element_type=jnp.float32)
    step_term = jnp.dot(block, w_mamba_dt, preferred_element_type=jnp.float32)
    terms = jnp.concatenate(
        [main_term.astype(jnp.bfloat16), step_term.astype(jnp.bfloat16),
         hi_lo(squares_mix.reshape(requests * steps))[:, : SQUARE_COLUMNS - w_mamba_dt.shape[1]]],
        axis=1,
    )
    own_rows = requests // devices
    own_terms = gather_sum(terms.reshape(devices, own_rows * steps, -1), "attn")
    own_scale_mix = scale_from(own_terms[:, mix_cols] + own_terms[:, mix_cols + 1], layer_width)
    own_terms = (own_terms[:, :mix_cols] * own_scale_mix[:, None]).reshape(own_rows, steps, mix_cols)
    main_part = own_terms[..., :main_cols].reshape(own_rows, steps, groups_local, -1)
    dt_raw = own_terms[..., main_cols:]

    def one_request(one_main, one_dt, one_conv, one_state):
        return mamba_core(
            one_main,
            one_dt,
            one_conv,
            one_state,
            conv_weight,
            conv_bias,
            a_log,
            dt_bias,
            skip_gain,
            group_gain,
        )

    mixer = jax.vmap(one_request)(main_part, dt_raw, conv_state, ssm_state)
    every_mixer = spread(mixer.reshape(own_rows * steps, -1), "attn")
    mixed_result = jnp.dot(
        every_mixer.reshape(requests * steps, -1), w_mamba_out, preferred_element_type=jnp.float32
    ).reshape(requests, steps, local_width)
    second = (first.astype(jnp.float32) + tp_sum(mixed_result)).astype(jnp.bfloat16)
    squares_ff = local_squares(second)
    normed_ff = gained(second, mlp_gain)
    flat_ff = normed_ff.reshape(requests * steps, local_width)
    up_local = jnp.dot(flat_ff, w_up, preferred_element_type=jnp.float32).astype(jnp.bfloat16)
    up_cols = up_local.shape[1]
    up_local = jnp.concatenate([up_local, hi_lo(squares_ff.reshape(requests * steps))], axis=1)
    own_up = gather_sum(up_local.reshape(devices, own_rows * steps, -1), "attn")
    scale_ff = scale_from(own_up[:, up_cols] + own_up[:, up_cols + 1], layer_width)
    active = spread(squared_relu(own_up[:, :up_cols] * scale_ff[:, None]), "attn")
    downward = jnp.dot(
        active.reshape(requests * steps, -1), w_down, preferred_element_type=jnp.float32
    ).reshape(requests, steps, local_width)
    return (second.astype(jnp.float32) + tp_sum(downward)).astype(jnp.bfloat16)


def solution(mesh):
    in_specs = (
        P(None, None, "attn"),
        P(),
        P(),
        P("attn", None, None, "tp"),
        P("attn"),
        P("attn", "tp"),
        P("attn", "tp"),
        P("attn", "tp"),
        P("tp", "attn"),
        P("attn"),
        P("attn", "tp", None),
        P("attn", "tp"),
        P("tp", "attn"),
        P(None, "tp", None),
        P("tp", None),
        P("attn", None, "tp", None),
        P("attn", "tp", None, None),
        P("tp"),
        P("tp"),
        P("tp"),
        P("tp", None),
        P("attn"),
        P("attn", "tp"),
        P("tp", "attn"),
    )
    out_specs = P(None, None, "attn")
    return jax.shard_map(
        on_device, mesh=mesh, in_specs=in_specs, out_specs=out_specs, check_vma=False
    )
```

```python
import jax
import jax.numpy as jnp
from jax import lax
from jax.experimental import pallas as pl
from jax.experimental.pallas import tpu as pltpu
from jax.sharding import PartitionSpec as P

HEAD_SIZE = 128
EPS = 1e-05
MASKED = -1e30
LANES = 128
STEPS = 2
REQ = 32
ROWS = REQ * STEPS
ATTN = 32
TP = 8
WIDTH = 8192
QKV_HALF = 768
UP_QUARTER = 512
MIX_QUARTER = 1280
FF_QUARTER = 640
INNER = 2048
STATES = 256
HEADS = 32
F32 = jnp.float32
BF16 = jnp.bfloat16


def dot(a, b):
    return jnp.dot(a, b, preferred_element_type=F32)


def iota(shape, axis):
    return lax.broadcasted_iota(jnp.int32, shape, axis)


def one_hot(condition):
    return jnp.where(condition, 1.0, 0.0).astype(BF16)


def gain_rows(x, gain):
    squares = jnp.sum(x * x, axis=-1, keepdims=True)
    high = squares.astype(BF16).astype(F32)
    column = iota((x.shape[0], LANES), 1)
    tile = jnp.where(column == 0, high, jnp.where(column == 1, squares - high, 0.0))
    return (x * gain).astype(BF16), tile.astype(BF16)


def scale_of(tile):
    return lax.rsqrt((tile[:, 0:1] + tile[:, 1:2]) / WIDTH + EPS)


def sum_pieces(ref, pieces):
    rows = ref.shape[0] // pieces
    return jnp.sum(ref[...].astype(F32).reshape(pieces, rows, ref.shape[1]), axis=0)


def write_copies(ref, piece, copies):
    piece = piece.astype(ref.dtype)
    for k in range(copies):
        ref[pl.ds(k * piece.shape[0], piece.shape[0]), :] = piece


def slots_by_row(slot_ref, columns):
    request = iota((REQ, columns), 0)
    column = iota((REQ, columns), 1)
    spread = one_hot((column % ROWS) // STEPS == request)
    slots = jnp.broadcast_to(slot_ref[...], (8, REQ)).astype(F32).astype(BF16)
    return dot(slots, spread)[0:1].astype(jnp.int32)


def qkv_kernel(hidden, slot_of, gain, w_query, w_key, w_value, out):
    normed, tile = gain_rows(hidden[...].astype(F32), gain[...])
    key = dot(normed, w_key[...]).astype(BF16)
    value = dot(normed, w_value[...]).astype(BF16)
    query = dot(normed, w_query[...]).astype(BF16)
    spare = jnp.zeros_like(tile)
    second = jnp.concatenate([query[:, QKV_HALF:], key, value, tile, spare], axis=1)
    halves = jnp.concatenate([query[:, :QKV_HALF], second], axis=0)
    column = iota((1, 2 * ROWS), 1)
    code = slots_by_row(slot_of, 2 * ROWS) * 4 + (column // ROWS) * 2 + column % STEPS
    row = iota((ATTN * 8, 2 * ROWS), 0)
    row_code = ((row // 8) * 2 + (row // 2) % 2) * 4 + ((row // 4) % 2) * 2 + row % 2
    out[...] = dot(one_hot(row_code == code), halves).astype(BF16)


def attend_kernel(pieces, lengths, slot_of, cache, out):
    first_slot = lax.axis_index("attn") * 2
    summed = sum_pieces(pieces, ATTN)
    low, high = summed[0:4], summed[4:8]
    scale = scale_of(high[:, 512 : 512 + LANES])
    low = (low * scale).astype(BF16).astype(F32)
    high = (high * scale).astype(BF16).astype(F32)
    whole = jnp.concatenate([low, high], axis=1)
    heads = 8
    factor = HEAD_SIZE ** (-0.5)
    group = heads * STEPS
    step_of_row = iota((group, 1), 0) % STEPS
    outputs = []
    for slot in range(2):
        length = jnp.int32(0)
        for r in range(REQ):
            length = length + jnp.where(slot_of[r] == first_slot + slot, lengths[r], 0)
        rows = whole[slot * 2 : slot * 2 + 2]
        query = jnp.concatenate([rows[:, h * LANES : (h + 1) * LANES] for h in range(heads)], axis=0)
        fresh_key = rows[:, 1024 : 1024 + LANES]
        fresh_value = rows[:, 1024 + LANES : 1024 + 2 * LANES]
        scores = (
            lax.dot_general(
                query.astype(BF16), cache[slot, 0], (((1,), (1,)), ((), ())), preferred_element_type=F32
            )
            * factor
        )
        scores = jnp.where(iota(scores.shape, 1) < length, scores, MASKED)
        fresh = []
        for t in range(STEPS):
            score = jnp.sum(query * fresh_key[t : t + 1], axis=-1, keepdims=True) * factor
            fresh.append(jnp.where(step_of_row >= t, score, MASKED))
        top = jnp.maximum(jnp.max(scores, axis=-1, keepdims=True), jnp.maximum(fresh[0], fresh[1]))
        weights = jnp.exp(scores - top)
        total = jnp.sum(weights, axis=-1, keepdims=True)
        mixed = dot(weights.astype(BF16), cache[slot, 1])
        for t in range(STEPS):
            weight = jnp.exp(fresh[t] - top)
            total = total + weight
            mixed = mixed + weight.astype(BF16).astype(F32) * fresh_value[t : t + 1]
        outputs.append(mixed / total)
    halves = []
    for half in range(2):
        for slot in range(2):
            part = outputs[slot]
            first = half * 4
            halves.append(
                jnp.concatenate([part[(first + h) * 2 : (first + h) * 2 + 2] for h in range(4)], axis=1)
            )
    write_copies(out, jnp.concatenate(halves, axis=0), ATTN)


def attn_out_kernel(pieces, slot_of, weight, out):
    column = iota((1, ROWS), 1)
    slots = slots_by_row(slot_of, ROWS) * 4 + column % STEPS
    row = iota((ATTN * 8, ROWS), 0)
    row_code = ((row // 8) * 2 + (row // 2) % 2) * 4 + ((row // 4) % 2) * 2 + row % 2
    gathered = pieces[...]
    total = None
    for half in range(2):
        chosen = one_hot(row_code == slots + half * 2)
        mine = lax.dot_general(chosen, gathered, (((0,), (0,)), ((), ())), preferred_element_type=F32)
        term = dot(mine.astype(BF16), weight[pl.ds(half * 512, 512), :])
        total = term if total is None else total + term
    write_copies(out, total, TP)


def by_owner(quarters):
    stacked = jnp.concatenate(quarters, axis=0)
    row = iota((ATTN * 8, 4 * ROWS), 0)
    column = iota((ATTN * 8, 4 * ROWS), 1)
    source = ((row // 2) % 4) * ROWS + (row // 8) * 2 + row % 2
    return dot(one_hot(source == column), stacked).astype(BF16)


def mix_in_kernel(pieces, hidden, gain, w_main, w_step, out, first_out):
    first = (sum_pieces(pieces, TP) + hidden[...].astype(F32)).astype(BF16)
    first_out[...] = first
    normed, tile = gain_rows(first.astype(F32), gain[...])
    main = dot(normed, w_main[...]).astype(BF16)
    steps = dot(normed, w_step[...]).astype(BF16)
    spare = jnp.zeros_like(tile)
    steps = jnp.concatenate([steps, spare[:, : LANES - HEADS]], axis=1)
    state = 2 * INNER
    extra = (
        [main[:, state : state + STATES]],
        [main[:, state + STATES : state + 2 * STATES]],
        [steps, tile],
        [spare, spare],
    )
    quarters = []
    for q in range(4):
        cut = slice(q * 512, (q + 1) * 512)
        parts = [main[:, :INNER][:, cut], main[:, INNER : 2 * INNER][:, cut]]
        quarters.append(jnp.concatenate(parts + extra[q], axis=1))
    out[...] = by_owner(quarters)


def silu(x):
    return x / (1.0 + jnp.exp(-x))


def mamba_kernel(
    pieces, conv_weight, conv_bias, conv_state, state, a_log, dt_bias, skip_gain, group_gain, out
):
    summed = sum_pieces(pieces, ATTN)
    scale = scale_of(summed[4:6, 1024 + LANES :])
    summed = summed * jnp.concatenate([scale] * 4, axis=0)

    def conved(now, cut):
        window = jnp.concatenate([conv_state[:, cut], now], axis=0)
        total = conv_bias[:, cut]
        for k in range(4):
            total = total + conv_weight[k : k + 1, cut] * window[k : k + 2]
        return silu(total)

    xs = jnp.concatenate(
        [
            conved(summed[q * 2 : q * 2 + 2, 512:1024], slice(q * 512, (q + 1) * 512))
            for q in range(4)
        ],
        axis=1,
    )
    b_in = conved(summed[0:2, 1024:1280], slice(INNER, INNER + STATES))
    c_out = conved(summed[2:4, 1024:1280], slice(INNER + STATES, INNER + 2 * STATES))
    gate = jnp.concatenate([summed[q * 2 : q * 2 + 2, 0:512] for q in range(4)], axis=1)
    raw = summed[4:6, 1024 : 1024 + HEADS] + dt_bias[...]
    step = jnp.maximum(raw, 0.0) + jnp.log1p(jnp.exp(-jnp.abs(raw)))
    decay = jnp.exp(-step * jnp.exp(a_log[...]))
    d0, d1, s0, s1 = decay[0:1], decay[1:2], step[0:1], step[1:2]
    per_head = jnp.concatenate([d0, d0 * d1, s0, d1 * s0, s1, skip_gain[...], d0, d0], axis=0)
    spread = jnp.where(iota((HEADS, INNER), 1) // 64 == iota((HEADS, INNER), 0), 1.0, 0.0)
    wide = jnp.dot(per_head, spread, precision=lax.Precision.HIGHEST, preferred_element_type=F32)
    c_high = c_out.astype(BF16)
    c_low = (c_out - c_high.astype(F32)).astype(BF16)
    whole = state[...]
    high = whole.astype(BF16)
    low = (whole - high.astype(F32)).astype(BF16)
    last = (((1,), (1,)), ((), ()))
    both = jnp.concatenate([c_high, c_low], axis=0)
    by_high = lax.dot_general(both, high, last, preferred_element_type=F32)
    by_low = lax.dot_general(c_high, low, last, preferred_element_type=F32)
    read_old = by_high[0:2] + by_high[2:4] + by_low
    b0c0 = jnp.sum(b_in[0:1] * c_out[0:1], axis=-1, keepdims=True)
    b0c1 = jnp.sum(b_in[0:1] * c_out[1:2], axis=-1, keepdims=True)
    b1c1 = jnp.sum(b_in[1:2] * c_out[1:2], axis=-1, keepdims=True)
    x0, x1 = xs[0:1], xs[1:2]
    read0 = wide[0:1] * read_old[0:1] + wide[2:3] * x0 * b0c0
    read1 = wide[1:2] * read_old[1:2] + wide[3:4] * x0 * b0c1 + wide[4:5] * x1 * b1c1
    read = jnp.concatenate([read0, read1], axis=0) + wide[5:6] * xs
    gated = read * silu(gate)
    mixer = gated * lax.rsqrt(jnp.mean(gated * gated, axis=-1, keepdims=True) + EPS) * group_gain[...]
    piece = jnp.concatenate([mixer[:, q * 512 : (q + 1) * 512] for q in range(4)], axis=0)
    write_copies(out, piece, ATTN)


def project_out_kernel(pieces, weight, out):
    row = iota((4 * ROWS, ATTN * 8), 0)
    column = iota((4 * ROWS, ATTN * 8), 1)
    source = ((row % ROWS) // 2) * 8 + (row // ROWS) * 2 + row % 2
    ordered = dot(one_hot(source == column), pieces[...]).astype(BF16)
    total = None
    for q in range(4):
        term = dot(ordered[q * ROWS : (q + 1) * ROWS], weight[pl.ds(q * 512, 512), :])
        total = term if total is None else total + term
    write_copies(out, total, TP)


def up_kernel(pieces, first, gain, w_up, out, second_out):
    second = (sum_pieces(pieces, TP) + first[...].astype(F32)).astype(BF16)
    second_out[...] = second
    normed, tile = gain_rows(second.astype(F32), gain[...])
    up = dot(normed, w_up[...]).astype(BF16)
    out[...] = by_owner(
        [
            jnp.concatenate([up[:, q * UP_QUARTER : (q + 1) * UP_QUARTER], tile], axis=1)
            for q in range(4)
        ]
    )


def active_kernel(pieces, out):
    summed = sum_pieces(pieces, ATTN)
    lifted = jnp.maximum(summed[:, :UP_QUARTER] * scale_of(summed[:, UP_QUARTER:]), 0.0)
    write_copies(out, lifted * lifted, ATTN)


def last_kernel(pieces, second, out):
    out[...] = (sum_pieces(pieces, TP) + second[...].astype(F32)).astype(BF16)


def call(kernel, out_shapes, *operands, smem=()):
    vmem = pl.BlockSpec(memory_space=pltpu.VMEM)
    scalar = pl.BlockSpec(memory_space=pltpu.SMEM)
    shapes = [jax.ShapeDtypeStruct(shape, BF16) for shape in out_shapes]
    return pl.pallas_call(
        kernel,
        out_shape=shapes[0] if len(shapes) == 1 else shapes,
        in_specs=[scalar if k in smem else vmem for k in range(len(operands))],
        out_specs=vmem if len(shapes) == 1 else [vmem] * len(shapes),
        compiler_params=pltpu.CompilerParams(vmem_limit_bytes=24 * 1024 * 1024),
    )(*operands)


def exchange(values, axis, pieces):
    rows, columns = values.shape
    cut = values.reshape(pieces, rows // pieces, columns)
    return lax.all_to_all(cut, axis, 0, 0).reshape(rows, columns)


def on_device(
    hidden,
    lengths,
    slot_of,
    kv_cache,
    attn_gain,
    w_query,
    key_matrix,
    value_matrix,
    w_attn_out,
    mamba_gain,
    w_mamba_in,
    w_mamba_dt,
    w_mamba_out,
    conv_weight,
    conv_bias,
    conv_state,
    ssm_state,
    a_log,
    dt_bias,
    skip_gain,
    group_gain,
    mlp_gain,
    w_up,
    w_down,
):
    rows = hidden.reshape(ROWS, -1)
    width = rows.shape[1]
    slot_row = slot_of.reshape(1, REQ)
    owned = ATTN * 8

    def row(x):
        return x.reshape(1, -1)

    pieces = call(
        qkv_kernel, [(owned, QKV_HALF)],
        rows, slot_row, row(attn_gain), w_query, key_matrix, value_matrix,
    )
    pieces = exchange(pieces, "attn", ATTN)
    pieces = call(
        attend_kernel, [(owned, 512)], pieces, lengths, slot_of, kv_cache, smem=(1, 2)
    )
    pieces = exchange(pieces, "attn", ATTN)
    pieces = call(attn_out_kernel, [(TP * ROWS, width)], pieces, slot_row, w_attn_out)
    pieces = exchange(pieces, "tp", TP)
    pieces, first = call(
        mix_in_kernel, [(owned, MIX_QUARTER), (ROWS, width)],
        pieces, rows, row(mamba_gain), w_mamba_in.reshape(width, -1), w_mamba_dt,
    )
    pieces = exchange(pieces, "attn", ATTN)
    pieces = call(
        mamba_kernel, [(owned, 512)],
        pieces, conv_weight.reshape(4, -1), conv_bias, conv_state.reshape(3, -1),
        ssm_state.reshape(INNER, STATES), row(a_log), row(dt_bias), row(skip_gain), group_gain,
    )
    pieces = exchange(pieces, "attn", ATTN)
    pieces = call(project_out_kernel, [(TP * ROWS, width)], pieces, w_mamba_out)
    pieces = exchange(pieces, "tp", TP)
    pieces, second = call(
        up_kernel, [(owned, FF_QUARTER), (ROWS, width)], pieces, first, row(mlp_gain), w_up
    )
    pieces = exchange(pieces, "attn", ATTN)
    pieces = call(active_kernel, [(owned, 512)], pieces)
    pieces = exchange(pieces, "attn", ATTN)
    pieces = call(project_out_kernel, [(TP * ROWS, width)], pieces, w_down)
    pieces = exchange(pieces, "tp", TP)
    return call(last_kernel, [(ROWS, width)], pieces, second).reshape(hidden.shape)


def solution(mesh):
    in_specs = (
        P(None, None, "attn"),
        P(),
        P(),
        P("attn", None, None, "tp"),
        P("attn"),
        P("attn", "tp"),
        P("attn", "tp"),
        P("attn", "tp"),
        P("tp", "attn"),
        P("attn"),
        P("attn", "tp", None),
        P("attn", "tp"),
        P("tp", "attn"),
        P(None, "tp", None),
        P("tp", None),
        P("attn", None, "tp", None),
        P("attn", "tp", None, None),
        P("tp"),
        P("tp"),
        P("tp"),
        P("tp", None),
        P("attn"),
        P("attn", "tp"),
        P("tp", "attn"),
    )
    out_specs = P(None, None, "attn")
    return jax.shard_map(
        on_device, mesh=mesh, in_specs=in_specs, out_specs=out_specs, check_vma=False
    )
```

```python
import jax
import jax.numpy as jnp
from jax import lax
from jax.experimental import pallas as pl
from jax.experimental.pallas import tpu as pltpu
from jax.sharding import PartitionSpec as P

HEAD_SIZE = 128
EPS = 1e-05
MASKED = -1e30
LANES = 128
STEPS = 2
REQ = 32
ROWS = REQ * STEPS
ATTN = 32
TP = 8
WIDTH = 8192
QKV_HALF = 768
UP_QUARTER = 512
MIX_QUARTER = 1280
FF_QUARTER = 640
INNER = 2048
STATES = 256
HEADS = 32
F32 = jnp.float32
BF16 = jnp.bfloat16


def dot(a, b):
    return jnp.dot(a, b, preferred_element_type=F32)


def iota(shape, axis):
    return lax.broadcasted_iota(jnp.int32, shape, axis)


def one_hot(condition):
    return jnp.where(condition, 1.0, 0.0).astype(BF16)


def gain_rows(x, gain):
    squares = jnp.sum(x * x, axis=-1, keepdims=True)
    high = squares.astype(BF16).astype(F32)
    column = iota((x.shape[0], LANES), 1)
    tile = jnp.where(column == 0, high, jnp.where(column == 1, squares - high, 0.0))
    return (x * gain).astype(BF16), tile.astype(BF16)


def scale_of(tile):
    return lax.rsqrt((tile[:, 0:1] + tile[:, 1:2]) / WIDTH + EPS)


def sum_pieces(ref, pieces):
    rows = ref.shape[0] // pieces
    return jnp.sum(ref[...].astype(F32).reshape(pieces, rows, ref.shape[1]), axis=0)


def write_copies(ref, piece, copies):
    piece = piece.astype(ref.dtype)
    for k in range(copies):
        ref[pl.ds(k * piece.shape[0], piece.shape[0]), :] = piece


def slots_by_row(slot_ref, columns):
    request = iota((REQ, columns), 0)
    column = iota((REQ, columns), 1)
    spread = one_hot((column % ROWS) // STEPS == request)
    slots = jnp.broadcast_to(slot_ref[...], (8, REQ)).astype(F32).astype(BF16)
    return dot(slots, spread)[0:1].astype(jnp.int32)


def qkv_kernel(
    hidden, gain, slot_of, lengths, w_key, w_value, w_query, cache,
    out, rows_out, slots_out, lengths_out, cache_out, *scratch
):
    places = (*scratch[:2], slots_out, lengths_out, *scratch[2:5], cache_out)
    copies = []
    for k, source in enumerate((hidden, gain, slot_of, lengths, w_key, w_value, w_query, cache)):
        copies.append(pltpu.make_async_copy(source, places[k], scratch[5].at[k]))
        copies[k].start()
    hidden_here, gain_here, key_here, value_here, query_here = scratch[:5]
    copies[0].wait()
    rows = hidden_here[...].astype(F32).reshape(ROWS, -1)
    rows_out[...] = rows.astype(BF16)
    copies[1].wait()
    normed, tile = gain_rows(rows, gain_here[...])
    for k in range(2, 7):
        copies[k].wait()
    key = dot(normed, key_here[...]).astype(BF16)
    value = dot(normed, value_here[...]).astype(BF16)
    query = dot(normed, query_here[...]).astype(BF16)
    spare = jnp.zeros_like(tile)
    second = jnp.concatenate([query[:, QKV_HALF:], key, value, tile, spare], axis=1)
    halves = jnp.concatenate([query[:, :QKV_HALF], second], axis=0)
    column = iota((1, 2 * ROWS), 1)
    code = slots_by_row(slots_out, 2 * ROWS) * 4 + (column // ROWS) * 2 + column % STEPS
    row = iota((ATTN * 8, 2 * ROWS), 0)
    row_code = ((row // 8) * 2 + (row // 2) % 2) * 4 + ((row // 4) % 2) * 2 + row % 2
    out[...] = dot(one_hot(row_code == code), halves).astype(BF16)
    copies[7].wait()


def attend_kernel(pieces, lengths, slot_of, cache, out):
    first_slot = lax.axis_index("attn") * 2
    summed = sum_pieces(pieces, ATTN)
    low, high = summed[0:4], summed[4:8]
    scale = scale_of(high[:, 512 : 512 + LANES])
    low = (low * scale).astype(BF16).astype(F32)
    high = (high * scale).astype(BF16).astype(F32)
    whole = jnp.concatenate([low, high], axis=1)
    heads = 8
    factor = HEAD_SIZE ** (-0.5)
    group = heads * STEPS
    step_of_row = iota((group, 1), 0) % STEPS
    outputs = []
    for slot in range(2):
        mine = slot_of[...] == first_slot + slot
        length = jnp.sum(jnp.where(mine, lengths[...].astype(F32), 0.0), axis=1, keepdims=True)
        length = length.astype(jnp.int32)
        rows = whole[slot * 2 : slot * 2 + 2]
        query = jnp.concatenate([rows[:, h * LANES : (h + 1) * LANES] for h in range(heads)], axis=0)
        fresh_key = rows[:, 1024 : 1024 + LANES]
        fresh_value = rows[:, 1024 + LANES : 1024 + 2 * LANES]
        scores = (
            lax.dot_general(
                query.astype(BF16), cache[slot, 0], (((1,), (1,)), ((), ())), preferred_element_type=F32
            )
            * factor
        )
        scores = jnp.where(iota(scores.shape, 1) < length, scores, MASKED)
        fresh = []
        for t in range(STEPS):
            score = jnp.sum(query * fresh_key[t : t + 1], axis=-1, keepdims=True) * factor
            fresh.append(jnp.where(step_of_row >= t, score, MASKED))
        top = jnp.maximum(jnp.max(scores, axis=-1, keepdims=True), jnp.maximum(fresh[0], fresh[1]))
        weights = jnp.exp(scores - top)
        total = jnp.sum(weights, axis=-1, keepdims=True)
        mixed = dot(weights.astype(BF16), cache[slot, 1])
        for t in range(STEPS):
            weight = jnp.exp(fresh[t] - top)
            total = total + weight
            mixed = mixed + weight.astype(BF16).astype(F32) * fresh_value[t : t + 1]
        outputs.append(mixed / total)
    halves = []
    for half in range(2):
        for slot in range(2):
            part = outputs[slot]
            first = half * 4
            halves.append(
                jnp.concatenate([part[(first + h) * 2 : (first + h) * 2 + 2] for h in range(4)], axis=1)
            )
    write_copies(out, jnp.concatenate(halves, axis=0), ATTN)


def attn_out_kernel(pieces, slot_of, weight, out):
    column = iota((1, ROWS), 1)
    slots = slots_by_row(slot_of, ROWS) * 4 + column % STEPS
    row = iota((ATTN * 8, ROWS), 0)
    row_code = ((row // 8) * 2 + (row // 2) % 2) * 4 + ((row // 4) % 2) * 2 + row % 2
    gathered = pieces[...]
    total = None
    for half in range(2):
        chosen = one_hot(row_code == slots + half * 2)
        mine = lax.dot_general(chosen, gathered, (((0,), (0,)), ((), ())), preferred_element_type=F32)
        term = dot(mine.astype(BF16), weight[pl.ds(half * 512, 512), :])
        total = term if total is None else total + term
    write_copies(out, total, TP)


def by_owner(quarters):
    stacked = jnp.concatenate(quarters, axis=0)
    row = iota((ATTN * 8, 4 * ROWS), 0)
    column = iota((ATTN * 8, 4 * ROWS), 1)
    source = ((row // 2) % 4) * ROWS + (row // 8) * 2 + row % 2
    return dot(one_hot(source == column), stacked).astype(BF16)


def mix_in_kernel(pieces, hidden, gain, w_main, w_step, out, first_out):
    first = (sum_pieces(pieces, TP) + hidden[...].astype(F32)).astype(BF16)
    first_out[...] = first
    normed, tile = gain_rows(first.astype(F32), gain[...])
    main = dot(normed, w_main[...]).astype(BF16)
    steps = lax.dot_general(
        normed, w_step[...], (((1,), (1,)), ((), ())), preferred_element_type=F32
    ).astype(BF16)
    spare = jnp.zeros_like(tile)
    steps = jnp.concatenate([steps, spare[:, : LANES - HEADS]], axis=1)
    state = 2 * INNER
    extra = (
        [main[:, state : state + STATES]],
        [main[:, state + STATES : state + 2 * STATES]],
        [steps, tile],
        [spare, spare],
    )
    quarters = []
    for q in range(4):
        cut = slice(q * 512, (q + 1) * 512)
        parts = [main[:, :INNER][:, cut], main[:, INNER : 2 * INNER][:, cut]]
        quarters.append(jnp.concatenate(parts + extra[q], axis=1))
    out[...] = by_owner(quarters)


def silu(x):
    return x / (1.0 + jnp.exp(-x))


def mamba_kernel(
    pieces, conv_weight, conv_bias, conv_state, state, a_log, dt_bias, skip_gain, group_gain, out
):
    summed = sum_pieces(pieces, ATTN)
    scale = scale_of(summed[4:6, 1024 + LANES :])
    summed = summed * jnp.concatenate([scale] * 4, axis=0)

    def conved(now, cut):
        window = [conv_state[k, :, cut] for k in range(3)] + [now[0:1], now[1:2]]
        totals = []
        for s in range(STEPS):
            total = conv_bias[:, cut]
            for k in range(4):
                total = total + conv_weight[k, :, cut] * window[s + k]
            totals.append(total)
        return silu(jnp.concatenate(totals, axis=0))

    xs = jnp.concatenate(
        [
            conved(summed[q * 2 : q * 2 + 2, 512:1024], slice(q * 512, (q + 1) * 512))
            for q in range(4)
        ],
        axis=1,
    )
    b_in = conved(summed[0:2, 1024:1280], slice(INNER, INNER + STATES))
    c_out = conved(summed[2:4, 1024:1280], slice(INNER + STATES, INNER + 2 * STATES))
    gate = jnp.concatenate([summed[q * 2 : q * 2 + 2, 0:512] for q in range(4)], axis=1)
    raw = summed[4:6, 1024 : 1024 + HEADS] + dt_bias[...]
    step = jnp.maximum(raw, 0.0) + jnp.log1p(jnp.exp(-jnp.abs(raw)))
    decay = jnp.exp(-step * jnp.exp(a_log[...]))
    d0, d1, s0, s1 = decay[0:1], decay[1:2], step[0:1], step[1:2]
    per_head = jnp.concatenate([d0, d0 * d1, s0, d1 * s0, s1, skip_gain[...], d0, d0], axis=0)
    spread = jnp.where(iota((HEADS, INNER), 1) // 64 == iota((HEADS, INNER), 0), 1.0, 0.0)
    wide = jnp.dot(per_head, spread, precision=lax.Precision.HIGHEST, preferred_element_type=F32)
    c_high = c_out.astype(BF16)
    c_low = (c_out - c_high.astype(F32)).astype(BF16)
    whole = state[...]
    high = whole.astype(BF16)
    low = (whole - high.astype(F32)).astype(BF16)
    last = (((1,), (1,)), ((), ()))
    both = jnp.concatenate([c_high, c_low], axis=0)
    by_high = lax.dot_general(both, high, last, preferred_element_type=F32)
    by_low = lax.dot_general(c_high, low, last, preferred_element_type=F32)
    read_old = by_high[0:2] + by_high[2:4] + by_low
    b0c0 = jnp.sum(b_in[0:1] * c_out[0:1], axis=-1, keepdims=True)
    b0c1 = jnp.sum(b_in[0:1] * c_out[1:2], axis=-1, keepdims=True)
    b1c1 = jnp.sum(b_in[1:2] * c_out[1:2], axis=-1, keepdims=True)
    x0, x1 = xs[0:1], xs[1:2]
    read0 = wide[0:1] * read_old[0:1] + wide[2:3] * x0 * b0c0
    read1 = wide[1:2] * read_old[1:2] + wide[3:4] * x0 * b0c1 + wide[4:5] * x1 * b1c1
    read = jnp.concatenate([read0, read1], axis=0) + wide[5:6] * xs
    gated = read * silu(gate)
    mixer = gated * lax.rsqrt(jnp.mean(gated * gated, axis=-1, keepdims=True) + EPS) * group_gain[...]
    piece = jnp.concatenate([mixer[:, q * 512 : (q + 1) * 512] for q in range(4)], axis=0)
    write_copies(out, piece, ATTN)


def project_out_kernel(pieces, weight, out):
    row = iota((4 * ROWS, ATTN * 8), 0)
    column = iota((4 * ROWS, ATTN * 8), 1)
    source = ((row % ROWS) // 2) * 8 + (row // ROWS) * 2 + row % 2
    ordered = dot(one_hot(source == column), pieces[...]).astype(BF16)
    total = None
    for q in range(4):
        term = dot(ordered[q * ROWS : (q + 1) * ROWS], weight[pl.ds(q * 512, 512), :])
        total = term if total is None else total + term
    write_copies(out, total, TP)


def up_kernel(pieces, first, gain, w_up, out, second_out):
    second = (sum_pieces(pieces, TP) + first[...].astype(F32)).astype(BF16)
    second_out[...] = second
    normed, tile = gain_rows(second.astype(F32), gain[...])
    up = dot(normed, w_up[...]).astype(BF16)
    out[...] = by_owner(
        [
            jnp.concatenate([up[:, q * UP_QUARTER : (q + 1) * UP_QUARTER], tile], axis=1)
            for q in range(4)
        ]
    )


def active_kernel(pieces, out):
    summed = sum_pieces(pieces, ATTN)
    lifted = jnp.maximum(summed[:, :UP_QUARTER] * scale_of(summed[:, UP_QUARTER:]), 0.0)
    write_copies(out, lifted * lifted, ATTN)


def last_kernel(pieces, second, out):
    total = sum_pieces(pieces, TP) + second[...].astype(F32)
    out[...] = total.reshape(out.shape).astype(BF16)


def call(kernel, outs, *operands, near=False, scratch=(), cost=None):
    space = pltpu.HBM if near else pltpu.VMEM
    shapes = [
        jax.ShapeDtypeStruct(out, BF16) if isinstance(out, tuple) else
        jax.ShapeDtypeStruct(out.shape, out.dtype)
        for out in outs
    ]
    if cost is None:
        cost = sum(x.size * x.dtype.itemsize for x in operands)
    if near:
        operands = [pltpu.with_memory_space_constraint(x, pltpu.HBM) for x in operands]
    result = pl.pallas_call(
        kernel,
        out_shape=shapes,
        in_specs=[pl.BlockSpec(memory_space=space)] * len(operands),
        out_specs=[pl.BlockSpec(memory_space=pltpu.VMEM)] * len(shapes),
        scratch_shapes=scratch,
        cost_estimate=pl.CostEstimate(flops=0, bytes_accessed=cost, transcendentals=0),
        compiler_params=pltpu.CompilerParams(vmem_limit_bytes=24 * 1024 * 1024),
    )(*operands)
    return result[0] if len(shapes) == 1 else result


def exchange(values, axis, pieces):
    rows, columns = values.shape
    cut = values.reshape(pieces, rows // pieces, columns)
    return lax.all_to_all(cut, axis, 0, 0).reshape(rows, columns)


def on_device(
    hidden,
    lengths,
    slot_of,
    kv_cache,
    attn_gain,
    w_query,
    key_matrix,
    value_matrix,
    w_attn_out,
    mamba_gain,
    w_mamba_in,
    w_mamba_dt,
    w_mamba_out,
    conv_weight,
    conv_bias,
    conv_state,
    ssm_state,
    a_log,
    dt_bias,
    skip_gain,
    group_gain,
    mlp_gain,
    w_up,
    w_down,
):
    width = hidden.shape[2]
    slot_row = slot_of.reshape(1, REQ)
    owned = ATTN * 8

    def row(x):
        return x.reshape(1, -1)

    length_row = lengths.reshape(1, REQ)
    kept = (hidden, row(attn_gain), key_matrix, value_matrix, w_query)
    pieces, rows, slot_row, length_row, cache = call(
        qkv_kernel, [(owned, QKV_HALF), (ROWS, width), slot_row, length_row, kv_cache],
        hidden, row(attn_gain), slot_row, length_row, key_matrix, value_matrix, w_query, kv_cache,
        near=True,
        scratch=[pltpu.VMEM(x.shape, x.dtype) for x in kept] + [pltpu.SemaphoreType.DMA((8,))],
        cost=16 * 1024 * 1024,
    )
    pieces = exchange(pieces, "attn", ATTN)
    pieces = call(attend_kernel, [(owned, 512)], pieces, length_row, slot_row, cache)
    pieces = exchange(pieces, "attn", ATTN)
    pieces = call(attn_out_kernel, [(TP * ROWS, width)], pieces, slot_row, w_attn_out)
    pieces = exchange(pieces, "tp", TP)
    pieces, first = call(
        mix_in_kernel, [(owned, MIX_QUARTER), (ROWS, width)],
        pieces, rows, row(mamba_gain), w_mamba_in.reshape(width, -1), w_mamba_dt.T,
    )
    pieces = exchange(pieces, "attn", ATTN)
    pieces = call(
        mamba_kernel, [(owned, 512)],
        pieces, conv_weight, conv_bias, conv_state.reshape(3, 1, -1),
        ssm_state.reshape(INNER, STATES), row(a_log), row(dt_bias), row(skip_gain), group_gain,
    )
    pieces = exchange(pieces, "attn", ATTN)
    pieces = call(project_out_kernel, [(TP * ROWS, width)], pieces, w_mamba_out)
    pieces = exchange(pieces, "tp", TP)
    pieces, second = call(
        up_kernel, [(owned, FF_QUARTER), (ROWS, width)], pieces, first, row(mlp_gain), w_up
    )
    pieces = exchange(pieces, "attn", ATTN)
    pieces = call(active_kernel, [(owned, 512)], pieces)
    pieces = exchange(pieces, "attn", ATTN)
    pieces = call(project_out_kernel, [(TP * ROWS, width)], pieces, w_down)
    pieces = exchange(pieces, "tp", TP)
    return call(last_kernel, [hidden.shape], pieces, second)


def solution(mesh):
    in_specs = (
        P(None, None, "attn"),
        P(),
        P(),
        P("attn", None, None, "tp"),
        P("attn"),
        P("attn", "tp"),
        P("attn", "tp"),
        P("attn", "tp"),
        P("tp", "attn"),
        P("attn"),
        P("attn", "tp", None),
        P("attn", "tp"),
        P("tp", "attn"),
        P(None, "tp", None),
        P("tp", None),
        P("attn", None, "tp", None),
        P("attn", "tp", None, None),
        P("tp"),
        P("tp"),
        P("tp"),
        P("tp", None),
        P("attn"),
        P("attn", "tp"),
        P("tp", "attn"),
    )
    out_specs = P(None, None, "attn")
    return jax.shard_map(
        on_device, mesh=mesh, in_specs=in_specs, out_specs=out_specs, check_vma=False
    )
```

```python
import jax
import jax.numpy as jnp
from jax import lax
from jax.experimental import pallas as pl
from jax.experimental.pallas import tpu as pltpu
from jax.sharding import PartitionSpec as P

HEAD_SIZE = 128
EPS = 1e-05
MASKED = -1e30
LANES = 128
STEPS = 2
REQ = 32
ROWS = REQ * STEPS
ATTN = 32
TP = 8
WIDTH = 8192
SLOTS = 64
INNER = 2048
STATES = 256
HEADS = 32
F32 = jnp.float32
BF16 = jnp.bfloat16


def dot(a, b):
    return jnp.dot(a, b, preferred_element_type=F32)


def iota(shape, axis):
    return lax.broadcasted_iota(jnp.int32, shape, axis)


def one_hot(condition):
    return jnp.where(condition, 1.0, 0.0).astype(BF16)


def gain_rows(x, gain):
    squares = jnp.sum(x * x, axis=-1, keepdims=True)
    high = squares.astype(BF16).astype(F32)
    column = iota((x.shape[0], LANES), 1)
    tile = jnp.where(column == 0, high, jnp.where(column == 1, squares - high, 0.0))
    return (x * gain).astype(BF16), tile.astype(BF16)


def scale_of(tile):
    return lax.rsqrt((tile[:, 0:1] + tile[:, 1:2]) / WIDTH + EPS)


def sum_pieces(ref, pieces):
    rows = ref.shape[0] // pieces
    return jnp.sum(ref[...].astype(F32).reshape(pieces, rows, ref.shape[1]), axis=0)


def write_copies(ref, piece, copies):
    piece = piece.astype(ref.dtype)
    for k in range(copies):
        ref[pl.ds(k * piece.shape[0], piece.shape[0]), :] = piece


def slots_by_row(slot_ref, columns):
    request = iota((REQ, columns), 0)
    column = iota((REQ, columns), 1)
    spread = one_hot((column % ROWS) // STEPS == request)
    slots = jnp.broadcast_to(slot_ref[...], (8, REQ)).astype(F32).astype(BF16)
    return dot(slots, spread)[0:1].astype(jnp.int32)


def qkv_kernel(
    hidden, gain, slot_of, lengths, w_key, w_value, w_query, cache,
    out, rows_out, slots_out, lengths_out, cache_out, *scratch
):
    places = (*scratch[:2], slots_out, lengths_out, *scratch[2:5], cache_out)
    copies = []
    for k, source in enumerate((hidden, gain, slot_of, lengths, w_key, w_value, w_query, cache)):
        copies.append(pltpu.make_async_copy(source, places[k], scratch[5].at[k]))
        copies[k].start()
    hidden_here, gain_here, key_here, value_here, query_here = scratch[:5]
    copies[0].wait()
    rows = hidden_here[...].astype(F32).reshape(ROWS, -1)
    rows_out[...] = rows.astype(BF16)
    copies[1].wait()
    normed, tile = gain_rows(rows, gain_here[...])
    for k in range(2, 7):
        copies[k].wait()
    key = dot(normed, key_here[...]).astype(BF16)
    value = dot(normed, value_here[...]).astype(BF16)
    query = dot(normed, query_here[...]).astype(BF16)
    whole = jnp.concatenate([query, key, value, tile], axis=1)
    column = iota((1, ROWS), 1)
    code = slots_by_row(slots_out, ROWS) * 2 + column % STEPS
    chosen = one_hot(iota((2 * SLOTS, ROWS), 0) == code)
    out[...] = dot(chosen, whole).reshape(out.shape).astype(BF16)
    copies[7].wait()


def attend_kernel(pieces, lengths, slot_of, cache, out):
    first_slot = lax.axis_index("attn") * 2
    summed = jnp.sum(pieces[...].astype(F32), axis=0)
    keys_at = 8 * HEAD_SIZE
    columns = keys_at + 2 * HEAD_SIZE
    whole = (summed[:, :columns] * scale_of(summed[:, columns:])).astype(BF16).astype(F32)
    heads = 8
    factor = HEAD_SIZE ** (-0.5)
    group = heads * STEPS
    step_of_row = iota((group, 1), 0) % STEPS
    outputs = []
    for slot in range(2):
        mine = slot_of[...] == first_slot + slot
        length = jnp.sum(jnp.where(mine, lengths[...].astype(F32), 0.0), axis=1, keepdims=True)
        length = length.astype(jnp.int32)
        rows = whole[slot * 2 : slot * 2 + 2]
        query = jnp.concatenate([rows[:, h * LANES : (h + 1) * LANES] for h in range(heads)], axis=0)
        fresh_key = rows[:, keys_at : keys_at + HEAD_SIZE]
        fresh_value = rows[:, keys_at + HEAD_SIZE :]
        scores = (
            lax.dot_general(
                query.astype(BF16), cache[slot, 0], (((1,), (1,)), ((), ())), preferred_element_type=F32
            )
            * factor
        )
        scores = jnp.where(iota(scores.shape, 1) < length, scores, MASKED)
        fresh = []
        for t in range(STEPS):
            score = jnp.sum(query * fresh_key[t : t + 1], axis=-1, keepdims=True) * factor
            fresh.append(jnp.where(step_of_row >= t, score, MASKED))
        top = jnp.maximum(jnp.max(scores, axis=-1, keepdims=True), jnp.maximum(fresh[0], fresh[1]))
        weights = jnp.exp(scores - top)
        total = jnp.sum(weights, axis=-1, keepdims=True)
        mixed = dot(weights.astype(BF16), cache[slot, 1])
        for t in range(STEPS):
            weight = jnp.exp(fresh[t] - top)
            total = total + weight
            mixed = mixed + weight.astype(BF16).astype(F32) * fresh_value[t : t + 1]
        outputs.append(mixed / total)
    halves = []
    for half in range(2):
        for slot in range(2):
            part = outputs[slot]
            first = half * 4
            halves.append(
                jnp.concatenate([part[(first + h) * 2 : (first + h) * 2 + 2] for h in range(4)], axis=1)
            )
    write_copies(out, jnp.concatenate(halves, axis=0), ATTN)


def attn_out_kernel(pieces, slot_of, weight, out):
    column = iota((1, ROWS), 1)
    slots = slots_by_row(slot_of, ROWS) * 4 + column % STEPS
    row = iota((ATTN * 8, ROWS), 0)
    row_code = ((row // 8) * 2 + (row // 2) % 2) * 4 + ((row // 4) % 2) * 2 + row % 2
    gathered = pieces[...]
    total = None
    for half in range(2):
        chosen = one_hot(row_code == slots + half * 2)
        mine = lax.dot_general(chosen, gathered, (((0,), (0,)), ((), ())), preferred_element_type=F32)
        term = dot(mine.astype(BF16), weight[pl.ds(half * 512, 512), :])
        total = term if total is None else total + term
    write_copies(out, total, TP)


def mix_in_kernel(pieces, hidden, gain, w_main, w_step, out, first_out):
    first = (sum_pieces(pieces, TP) + hidden[...].astype(F32)).astype(BF16)
    first_out[...] = first
    normed, tile = gain_rows(first.astype(F32), gain[...])
    main = dot(normed, w_main[...])
    steps = lax.dot_general(
        normed, w_step[...], (((1,), (1,)), ((), ())), preferred_element_type=F32
    )
    both = jnp.concatenate([main, steps, tile[:, : LANES - HEADS].astype(F32)], axis=1)
    out[...] = both.reshape(out.shape).astype(BF16)


def silu(x):
    return x / (1.0 + jnp.exp(-x))


def mamba_kernel(
    pieces, conv_weight, conv_bias, conv_state, state, a_log, dt_bias, skip_gain, group_gain, out
):
    summed = jnp.sum(pieces[...].astype(F32), axis=0)
    state_at = 2 * INNER
    steps_at = state_at + 2 * STATES
    last = summed[:, steps_at:]
    summed = summed * scale_of(last[:, HEADS:])

    def conved(now, cut):
        window = [conv_state[k, :, cut] for k in range(3)] + [now[0:1], now[1:2]]
        totals = []
        for s in range(STEPS):
            total = conv_bias[:, cut]
            for k in range(4):
                total = total + conv_weight[k, :, cut] * window[s + k]
            totals.append(total)
        return silu(jnp.concatenate(totals, axis=0))

    xs = conved(summed[:, INNER:state_at], slice(0, INNER))
    b_in = conved(summed[:, state_at : state_at + STATES], slice(INNER, INNER + STATES))
    c_out = conved(summed[:, state_at + STATES : steps_at], slice(INNER + STATES, INNER + 2 * STATES))
    gate = summed[:, :INNER]
    raw = summed[:, steps_at : steps_at + HEADS] + dt_bias[...]
    step = jnp.maximum(raw, 0.0) + jnp.log1p(jnp.exp(-jnp.abs(raw)))
    decay = jnp.exp(-step * jnp.exp(a_log[...]))
    d0, d1, s0, s1 = decay[0:1], decay[1:2], step[0:1], step[1:2]
    per_head = jnp.concatenate([d0, d0 * d1, s0, d1 * s0, s1, skip_gain[...], d0, d0], axis=0)
    spread = jnp.where(iota((HEADS, INNER), 1) // 64 == iota((HEADS, INNER), 0), 1.0, 0.0)
    wide = jnp.dot(per_head, spread, precision=lax.Precision.HIGHEST, preferred_element_type=F32)
    c_high = c_out.astype(BF16)
    c_low = (c_out - c_high.astype(F32)).astype(BF16)
    whole = state[...]
    high = whole.astype(BF16)
    low = (whole - high.astype(F32)).astype(BF16)
    along = (((1,), (1,)), ((), ()))
    both = jnp.concatenate([c_high, c_low], axis=0)
    by_high = lax.dot_general(both, high, along, preferred_element_type=F32)
    by_low = lax.dot_general(c_high, low, along, preferred_element_type=F32)
    read_old = by_high[0:2] + by_high[2:4] + by_low
    b0c0 = jnp.sum(b_in[0:1] * c_out[0:1], axis=-1, keepdims=True)
    b0c1 = jnp.sum(b_in[0:1] * c_out[1:2], axis=-1, keepdims=True)
    b1c1 = jnp.sum(b_in[1:2] * c_out[1:2], axis=-1, keepdims=True)
    x0, x1 = xs[0:1], xs[1:2]
    read0 = wide[0:1] * read_old[0:1] + wide[2:3] * x0 * b0c0
    read1 = wide[1:2] * read_old[1:2] + wide[3:4] * x0 * b0c1 + wide[4:5] * x1 * b1c1
    read = jnp.concatenate([read0, read1], axis=0) + wide[5:6] * xs
    gated = read * silu(gate)
    mixer = gated * lax.rsqrt(jnp.mean(gated * gated, axis=-1, keepdims=True) + EPS) * group_gain[...]
    piece = jnp.concatenate([mixer[:, q * 512 : (q + 1) * 512] for q in range(4)], axis=0)
    write_copies(out, piece, ATTN)


def project_out_kernel(pieces, weight, out):
    row = iota((4 * ROWS, ATTN * 8), 0)
    column = iota((4 * ROWS, ATTN * 8), 1)
    source = ((row % ROWS) // 2) * 8 + (row // ROWS) * 2 + row % 2
    ordered = dot(one_hot(source == column), pieces[...]).astype(BF16)
    total = None
    for q in range(4):
        term = dot(ordered[q * ROWS : (q + 1) * ROWS], weight[pl.ds(q * 512, 512), :])
        total = term if total is None else total + term
    write_copies(out, total, TP)


def up_kernel(pieces, first, gain, w_up, out, second_out):
    second = (sum_pieces(pieces, TP) + first[...].astype(F32)).astype(BF16)
    second_out[...] = second
    normed, tile = gain_rows(second.astype(F32), gain[...])
    up = dot(normed, w_up[...])
    both = jnp.concatenate([up, tile.astype(F32)], axis=1)
    out[...] = both.reshape(out.shape).astype(BF16)


def active_kernel(pieces, out):
    summed = jnp.sum(pieces[...].astype(F32), axis=0)
    lifted = jnp.maximum(summed[:, :INNER] * scale_of(summed[:, INNER:]), 0.0)
    active = lifted * lifted
    piece = jnp.concatenate([active[:, q * 512 : (q + 1) * 512] for q in range(4)], axis=0)
    write_copies(out, piece, ATTN)


def last_kernel(pieces, second, out):
    total = sum_pieces(pieces, TP) + second[...].astype(F32)
    out[...] = total.reshape(out.shape).astype(BF16)


def call(kernel, outs, *operands, near=False, scratch=(), cost=None):
    space = pltpu.HBM if near else pltpu.VMEM
    shapes = [
        jax.ShapeDtypeStruct(out, BF16) if isinstance(out, tuple) else
        jax.ShapeDtypeStruct(out.shape, out.dtype)
        for out in outs
    ]
    if cost is None:
        cost = sum(x.size * x.dtype.itemsize for x in operands)
    if near:
        operands = [pltpu.with_memory_space_constraint(x, pltpu.HBM) for x in operands]
    result = pl.pallas_call(
        kernel,
        out_shape=shapes,
        in_specs=[pl.BlockSpec(memory_space=space)] * len(operands),
        out_specs=[pl.BlockSpec(memory_space=pltpu.VMEM)] * len(shapes),
        scratch_shapes=scratch,
        cost_estimate=pl.CostEstimate(flops=0, bytes_accessed=cost, transcendentals=0),
        compiler_params=pltpu.CompilerParams(vmem_limit_bytes=24 * 1024 * 1024),
    )(*operands)
    return result[0] if len(shapes) == 1 else result


def exchange(values, axis, pieces):
    rows, columns = values.shape
    cut = values.reshape(pieces, rows // pieces, columns)
    return lax.all_to_all(cut, axis, 0, 0).reshape(rows, columns)


def on_device(
    hidden,
    lengths,
    slot_of,
    kv_cache,
    attn_gain,
    w_query,
    key_matrix,
    value_matrix,
    w_attn_out,
    mamba_gain,
    w_mamba_in,
    w_mamba_dt,
    w_mamba_out,
    conv_weight,
    conv_bias,
    conv_state,
    ssm_state,
    a_log,
    dt_bias,
    skip_gain,
    group_gain,
    mlp_gain,
    w_up,
    w_down,
):
    width = hidden.shape[2]
    slot_row = slot_of.reshape(1, REQ)
    owned = ATTN * 8

    def row(x):
        return x.reshape(1, -1)

    length_row = lengths.reshape(1, REQ)
    kept = (hidden, row(attn_gain), key_matrix, value_matrix, w_query)
    pieces, rows, slot_row, length_row, cache = call(
        qkv_kernel, [(ATTN, 4, 1408), (ROWS, width), slot_row, length_row, kv_cache],
        hidden, row(attn_gain), slot_row, length_row, key_matrix, value_matrix, w_query, kv_cache,
        near=True,
        scratch=[pltpu.VMEM(x.shape, x.dtype) for x in kept] + [pltpu.SemaphoreType.DMA((8,))],
        cost=16 * 1024 * 1024,
    )
    pieces = lax.all_to_all(pieces, "attn", 0, 0)
    pieces = call(attend_kernel, [(owned, 512)], pieces, length_row, slot_row, cache)
    pieces = exchange(pieces, "attn", ATTN)
    pieces = call(attn_out_kernel, [(TP * ROWS, width)], pieces, slot_row, w_attn_out)
    pieces = exchange(pieces, "tp", TP)
    pieces, first = call(
        mix_in_kernel, [(ATTN, STEPS, 2 * INNER + 2 * STATES + LANES), (ROWS, width)],
        pieces, rows, row(mamba_gain), w_mamba_in.reshape(width, -1), w_mamba_dt.T,
    )
    pieces = lax.all_to_all(pieces, "attn", 0, 0)
    pieces = call(
        mamba_kernel, [(owned, 512)],
        pieces, conv_weight, conv_bias, conv_state.reshape(3, 1, -1),
        ssm_state.reshape(INNER, STATES), row(a_log), row(dt_bias), row(skip_gain), group_gain,
    )
    pieces = exchange(pieces, "attn", ATTN)
    pieces = call(project_out_kernel, [(TP * ROWS, width)], pieces, w_mamba_out)
    pieces = exchange(pieces, "tp", TP)
    pieces, second = call(
        up_kernel, [(ATTN, STEPS, INNER + LANES), (ROWS, width)], pieces, first, row(mlp_gain), w_up
    )
    pieces = lax.all_to_all(pieces, "attn", 0, 0)
    pieces = call(active_kernel, [(owned, 512)], pieces)
    pieces = exchange(pieces, "attn", ATTN)
    pieces = call(project_out_kernel, [(TP * ROWS, width)], pieces, w_down)
    pieces = exchange(pieces, "tp", TP)
    return call(last_kernel, [hidden.shape], pieces, second)


def solution(mesh):
    in_specs = (
        P(None, None, "attn"),
        P(),
        P(),
        P("attn", None, None, "tp"),
        P("attn"),
        P("attn", "tp"),
        P("attn", "tp"),
        P("attn", "tp"),
        P("tp", "attn"),
        P("attn"),
        P("attn", "tp", None),
        P("attn", "tp"),
        P("tp", "attn"),
        P(None, "tp", None),
        P("tp", None),
        P("attn", None, "tp", None),
        P("attn", "tp", None, None),
        P("tp"),
        P("tp"),
        P("tp"),
        P("tp", None),
        P("attn"),
        P("attn", "tp"),
        P("tp", "attn"),
    )
    out_specs = P(None, None, "attn")
    return jax.shard_map(
        on_device, mesh=mesh, in_specs=in_specs, out_specs=out_specs, check_vma=False
    )
```

```python
import jax
import jax.numpy as jnp
from jax import lax
from jax.experimental import pallas as pl
from jax.experimental.pallas import tpu as pltpu
from jax.sharding import PartitionSpec as P

HEAD_SIZE = 128
EPS = 1e-05
MASKED = -1e30
LANES = 128
STEPS = 2
REQ = 32
ROWS = REQ * STEPS
ATTN = 32
TP = 8
WIDTH = 8192
SLOTS = 64
INNER = 2048
STATES = 256
HEADS = 32
F32 = jnp.float32
BF16 = jnp.bfloat16


def dot(a, b):
    return jnp.dot(a, b, preferred_element_type=F32)


def iota(shape, axis):
    return lax.broadcasted_iota(jnp.int32, shape, axis)


def one_hot(condition):
    return jnp.where(condition, 1.0, 0.0).astype(BF16)


def gain_rows(x, gain):
    squares = jnp.sum(x * x, axis=-1, keepdims=True)
    high = squares.astype(BF16).astype(F32)
    column = iota((x.shape[0], LANES), 1)
    tile = jnp.where(column == 0, high, jnp.where(column == 1, squares - high, 0.0))
    return (x * gain).astype(BF16), tile.astype(BF16)


def scale_of(tile):
    return lax.rsqrt((tile[:, 0:1] + tile[:, 1:2]) / WIDTH + EPS)


def sum_pieces(ref, pieces):
    rows = ref.shape[0] // pieces
    return jnp.sum(ref[...].astype(F32).reshape(pieces, rows, ref.shape[1]), axis=0)


def write_copies(ref, piece, copies):
    piece = piece.astype(ref.dtype)
    for k in range(copies):
        ref[pl.ds(k * piece.shape[0], piece.shape[0]), :] = piece


def slots_by_row(slot_ref, columns):
    request = iota((REQ, columns), 0)
    column = iota((REQ, columns), 1)
    spread = one_hot((column % ROWS) // STEPS == request)
    slots = jnp.broadcast_to(slot_ref[...], (8, REQ)).astype(F32).astype(BF16)
    return dot(slots, spread)[0:1].astype(jnp.int32)


def qkv_kernel(
    hidden, gain, slot_of, lengths, w_key, w_value, w_query, cache,
    out, rows_out, slots_out, lengths_out, cache_out, *scratch
):
    places = (*scratch[:2], slots_out, lengths_out, *scratch[2:5], cache_out)
    copies = []
    for k, source in enumerate((hidden, gain, slot_of, lengths, w_key, w_value, w_query, cache)):
        copies.append(pltpu.make_async_copy(source, places[k], scratch[5].at[k]))
        copies[k].start()
    hidden_here, gain_here, key_here, value_here, query_here = scratch[:5]
    copies[0].wait()
    rows = hidden_here[...].astype(F32).reshape(ROWS, -1)
    rows_out[...] = rows.astype(BF16)
    copies[1].wait()
    normed, tile = gain_rows(rows, gain_here[...])
    for k in range(2, 7):
        copies[k].wait()
    key = dot(normed, key_here[...]).astype(BF16)
    value = dot(normed, value_here[...]).astype(BF16)
    query = dot(normed, query_here[...]).astype(BF16)
    whole = jnp.concatenate([query, key, value, tile], axis=1)
    column = iota((1, ROWS), 1)
    code = slots_by_row(slots_out, ROWS) * 2 + column % STEPS
    chosen = one_hot(iota((2 * SLOTS, ROWS), 0) == code)
    out[...] = dot(chosen, whole).reshape(out.shape).astype(BF16)
    copies[7].wait()


def attend_kernel(pieces, lengths, slot_of, cache, out):
    first_slot = lax.axis_index("attn") * 2
    summed = jnp.sum(pieces[...].astype(F32), axis=0)
    keys_at = 8 * HEAD_SIZE
    columns = keys_at + 2 * HEAD_SIZE
    whole = (summed[:, :columns] * scale_of(summed[:, columns:])).astype(BF16).astype(F32)
    heads = 8
    factor = HEAD_SIZE ** (-0.5)
    group = heads * STEPS
    step_of_row = iota((group, 1), 0) % STEPS
    outputs = []
    for slot in range(2):
        mine = slot_of[...] == first_slot + slot
        length = jnp.sum(jnp.where(mine, lengths[...].astype(F32), 0.0), axis=1, keepdims=True)
        length = length.astype(jnp.int32)
        rows = whole[slot * 2 : slot * 2 + 2]
        query = jnp.concatenate([rows[:, h * LANES : (h + 1) * LANES] for h in range(heads)], axis=0)
        fresh_key = rows[:, keys_at : keys_at + HEAD_SIZE]
        fresh_value = rows[:, keys_at + HEAD_SIZE :]
        scores = (
            lax.dot_general(
                query.astype(BF16), cache[slot, 0], (((1,), (1,)), ((), ())), preferred_element_type=F32
            )
            * factor
        )
        scores = jnp.where(iota(scores.shape, 1) < length, scores, MASKED)
        fresh = []
        for t in range(STEPS):
            score = jnp.sum(query * fresh_key[t : t + 1], axis=-1, keepdims=True) * factor
            fresh.append(jnp.where(step_of_row >= t, score, MASKED))
        top = jnp.maximum(jnp.max(scores, axis=-1, keepdims=True), jnp.maximum(fresh[0], fresh[1]))
        weights = jnp.exp(scores - top)
        total = jnp.sum(weights, axis=-1, keepdims=True)
        mixed = dot(weights.astype(BF16), cache[slot, 1])
        for t in range(STEPS):
            weight = jnp.exp(fresh[t] - top)
            total = total + weight
            mixed = mixed + weight.astype(BF16).astype(F32) * fresh_value[t : t + 1]
        outputs.append(mixed / total)
    halves = []
    for half in range(2):
        for slot in range(2):
            part = outputs[slot]
            first = half * 4
            halves.append(
                jnp.concatenate([part[(first + h) * 2 : (first + h) * 2 + 2] for h in range(4)], axis=1)
            )
    write_copies(out, jnp.concatenate(halves, axis=0), ATTN)


def pair_kernel(own, other, out):
    out[...] = (own[...].astype(F32) + other[...].astype(F32)).astype(BF16)


def sum_chips(own, second, before, after):
    here = own[...].astype(F32) + second[...].astype(F32)
    return here + (before[...].astype(F32) + after[...].astype(F32))


def attn_out_kernel(pieces, slot_of, weight, out):
    column = iota((1, ROWS), 1)
    slots = slots_by_row(slot_of, ROWS) * 4 + column % STEPS
    row = iota((ATTN * 8, ROWS), 0)
    row_code = ((row // 8) * 2 + (row // 2) % 2) * 4 + ((row // 4) % 2) * 2 + row % 2
    gathered = pieces[...]
    total = None
    for half in range(2):
        chosen = one_hot(row_code == slots + half * 2)
        mine = lax.dot_general(chosen, gathered, (((0,), (0,)), ((), ())), preferred_element_type=F32)
        term = dot(mine.astype(BF16), weight[pl.ds(half * 512, 512), :])
        total = term if total is None else total + term
    out[...] = total.astype(BF16)


def mix_in_kernel(own, second, before, after, hidden, gain, w_main, w_step, out, first_out):
    first = (sum_chips(own, second, before, after) + hidden[...].astype(F32)).astype(BF16)
    first_out[...] = first
    normed, tile = gain_rows(first.astype(F32), gain[...])
    main = dot(normed, w_main[...])
    steps = lax.dot_general(
        normed, w_step[...], (((1,), (1,)), ((), ())), preferred_element_type=F32
    )
    both = jnp.concatenate([main, steps, tile[:, : LANES - HEADS].astype(F32)], axis=1)
    out[...] = both.reshape(out.shape).astype(BF16)


def silu(x):
    return x / (1.0 + jnp.exp(-x))


def mamba_kernel(
    pieces, conv_weight, conv_bias, conv_state, state, a_log, dt_bias, skip_gain, group_gain, out
):
    summed = jnp.sum(pieces[...].astype(F32), axis=0)
    state_at = 2 * INNER
    steps_at = state_at + 2 * STATES
    last = summed[:, steps_at:]
    summed = summed * scale_of(last[:, HEADS:])

    def conved(now, cut):
        window = [conv_state[k, :, cut] for k in range(3)] + [now[0:1], now[1:2]]
        totals = []
        for s in range(STEPS):
            total = conv_bias[:, cut]
            for k in range(4):
                total = total + conv_weight[k, :, cut] * window[s + k]
            totals.append(total)
        return silu(jnp.concatenate(totals, axis=0))

    xs = conved(summed[:, INNER:state_at], slice(0, INNER))
    b_in = conved(summed[:, state_at : state_at + STATES], slice(INNER, INNER + STATES))
    c_out = conved(summed[:, state_at + STATES : steps_at], slice(INNER + STATES, INNER + 2 * STATES))
    gate = summed[:, :INNER]
    raw = summed[:, steps_at : steps_at + HEADS] + dt_bias[...]
    step = jnp.maximum(raw, 0.0) + jnp.log1p(jnp.exp(-jnp.abs(raw)))
    decay = jnp.exp(-step * jnp.exp(a_log[...]))
    d0, d1, s0, s1 = decay[0:1], decay[1:2], step[0:1], step[1:2]
    per_head = jnp.concatenate([d0, d0 * d1, s0, d1 * s0, s1, skip_gain[...], d0, d0], axis=0)
    spread = jnp.where(iota((HEADS, INNER), 1) // 64 == iota((HEADS, INNER), 0), 1.0, 0.0)
    wide = jnp.dot(per_head, spread, precision=lax.Precision.HIGHEST, preferred_element_type=F32)
    c_high = c_out.astype(BF16)
    c_low = (c_out - c_high.astype(F32)).astype(BF16)
    whole = state[...]
    high = whole.astype(BF16)
    low = (whole - high.astype(F32)).astype(BF16)
    along = (((1,), (1,)), ((), ()))
    both = jnp.concatenate([c_high, c_low], axis=0)
    by_high = lax.dot_general(both, high, along, preferred_element_type=F32)
    by_low = lax.dot_general(c_high, low, along, preferred_element_type=F32)
    read_old = by_high[0:2] + by_high[2:4] + by_low
    b0c0 = jnp.sum(b_in[0:1] * c_out[0:1], axis=-1, keepdims=True)
    b0c1 = jnp.sum(b_in[0:1] * c_out[1:2], axis=-1, keepdims=True)
    b1c1 = jnp.sum(b_in[1:2] * c_out[1:2], axis=-1, keepdims=True)
    x0, x1 = xs[0:1], xs[1:2]
    read0 = wide[0:1] * read_old[0:1] + wide[2:3] * x0 * b0c0
    read1 = wide[1:2] * read_old[1:2] + wide[3:4] * x0 * b0c1 + wide[4:5] * x1 * b1c1
    read = jnp.concatenate([read0, read1], axis=0) + wide[5:6] * xs
    gated = read * silu(gate)
    mixer = gated * lax.rsqrt(jnp.mean(gated * gated, axis=-1, keepdims=True) + EPS) * group_gain[...]
    piece = jnp.concatenate([mixer[:, q * 512 : (q + 1) * 512] for q in range(4)], axis=0)
    write_copies(out, piece, ATTN)


def project_out_kernel(pieces, weight, out):
    row = iota((4 * ROWS, ATTN * 8), 0)
    column = iota((4 * ROWS, ATTN * 8), 1)
    source = ((row % ROWS) // 2) * 8 + (row // ROWS) * 2 + row % 2
    ordered = dot(one_hot(source == column), pieces[...]).astype(BF16)
    total = None
    for q in range(4):
        term = dot(ordered[q * ROWS : (q + 1) * ROWS], weight[pl.ds(q * 512, 512), :])
        total = term if total is None else total + term
    out[...] = total.astype(BF16)


def up_kernel(own, opposite, before, after, first, gain, w_up, out, second_out):
    second = (sum_chips(own, opposite, before, after) + first[...].astype(F32)).astype(BF16)
    second_out[...] = second
    normed, tile = gain_rows(second.astype(F32), gain[...])
    up = dot(normed, w_up[...])
    both = jnp.concatenate([up, tile.astype(F32)], axis=1)
    out[...] = both.reshape(out.shape).astype(BF16)


def active_kernel(pieces, out):
    summed = jnp.sum(pieces[...].astype(F32), axis=0)
    lifted = jnp.maximum(summed[:, :INNER] * scale_of(summed[:, INNER:]), 0.0)
    active = lifted * lifted
    piece = jnp.concatenate([active[:, q * 512 : (q + 1) * 512] for q in range(4)], axis=0)
    write_copies(out, piece, ATTN)


def last_kernel(own, opposite, before, after, second, out):
    total = sum_chips(own, opposite, before, after) + second[...].astype(F32)
    out[...] = total.reshape(out.shape).astype(BF16)


def call(kernel, outs, *operands, near=False, scratch=(), cost=None):
    space = pltpu.HBM if near else pltpu.VMEM
    shapes = [
        jax.ShapeDtypeStruct(out, BF16) if isinstance(out, tuple) else
        jax.ShapeDtypeStruct(out.shape, out.dtype)
        for out in outs
    ]
    if cost is None:
        cost = sum(x.size * x.dtype.itemsize for x in operands)
    if near:
        operands = [pltpu.with_memory_space_constraint(x, pltpu.HBM) for x in operands]
    result = pl.pallas_call(
        kernel,
        out_shape=shapes,
        in_specs=[pl.BlockSpec(memory_space=space)] * len(operands),
        out_specs=[pl.BlockSpec(memory_space=pltpu.VMEM)] * len(shapes),
        scratch_shapes=scratch,
        cost_estimate=pl.CostEstimate(flops=0, bytes_accessed=cost, transcendentals=0),
        compiler_params=pltpu.CompilerParams(vmem_limit_bytes=24 * 1024 * 1024),
    )(*operands)
    return result[0] if len(shapes) == 1 else result


def exchange(values, axis, pieces):
    rows, columns = values.shape
    cut = values.reshape(pieces, rows // pieces, columns)
    return lax.all_to_all(cut, axis, 0, 0).reshape(rows, columns)


def over_tp(part):
    other = lax.ppermute(part, "tp", [(k, k ^ 1) for k in range(TP)])
    pair = call(pair_kernel, [part.shape], part, other)
    shifted = [lax.ppermute(pair, "tp", [(k, (k + s) % TP) for k in range(TP)]) for s in (4, 2, 6)]
    return [pair, *shifted]


def on_device(
    hidden,
    lengths,
    slot_of,
    kv_cache,
    attn_gain,
    w_query,
    key_matrix,
    value_matrix,
    w_attn_out,
    mamba_gain,
    w_mamba_in,
    w_mamba_dt,
    w_mamba_out,
    conv_weight,
    conv_bias,
    conv_state,
    ssm_state,
    a_log,
    dt_bias,
    skip_gain,
    group_gain,
    mlp_gain,
    w_up,
    w_down,
):
    width = hidden.shape[2]
    slot_row = slot_of.reshape(1, REQ)
    owned = ATTN * 8

    def row(x):
        return x.reshape(1, -1)

    length_row = lengths.reshape(1, REQ)
    kept = (hidden, row(attn_gain), key_matrix, value_matrix, w_query)
    pieces, rows, slot_row, length_row, cache = call(
        qkv_kernel, [(ATTN, 4, 1408), (ROWS, width), slot_row, length_row, kv_cache],
        hidden, row(attn_gain), slot_row, length_row, key_matrix, value_matrix, w_query, kv_cache,
        near=True,
        scratch=[pltpu.VMEM(x.shape, x.dtype) for x in kept] + [pltpu.SemaphoreType.DMA((8,))],
        cost=16 * 1024 * 1024,
    )
    pieces = lax.all_to_all(pieces, "attn", 0, 0)
    pieces = call(attend_kernel, [(owned, 512)], pieces, length_row, slot_row, cache)
    pieces = exchange(pieces, "attn", ATTN)
    pieces = call(attn_out_kernel, [(ROWS, width)], pieces, slot_row, w_attn_out)
    pieces = over_tp(pieces)
    pieces, first = call(
        mix_in_kernel, [(ATTN, STEPS, 2 * INNER + 2 * STATES + LANES), (ROWS, width)],
        *pieces, rows, row(mamba_gain), w_mamba_in.reshape(width, -1), w_mamba_dt.T,
    )
    pieces = lax.all_to_all(pieces, "attn", 0, 0)
    pieces = call(
        mamba_kernel, [(owned, 512)],
        pieces, conv_weight, conv_bias, conv_state.reshape(3, 1, -1),
        ssm_state.reshape(INNER, STATES), row(a_log), row(dt_bias), row(skip_gain), group_gain,
    )
    pieces = exchange(pieces, "attn", ATTN)
    pieces = call(project_out_kernel, [(ROWS, width)], pieces, w_mamba_out)
    pieces = over_tp(pieces)
    pieces, second = call(
        up_kernel, [(ATTN, STEPS, INNER + LANES), (ROWS, width)], *pieces, first, row(mlp_gain), w_up
    )
    pieces = lax.all_to_all(pieces, "attn", 0, 0)
    pieces = call(active_kernel, [(owned, 512)], pieces)
    pieces = exchange(pieces, "attn", ATTN)
    pieces = call(project_out_kernel, [(ROWS, width)], pieces, w_down)
    pieces = over_tp(pieces)
    return call(last_kernel, [hidden.shape], *pieces, second)


def solution(mesh):
    in_specs = (
        P(None, None, "attn"),
        P(),
        P(),
        P("attn", None, None, "tp"),
        P("attn"),
        P("attn", "tp"),
        P("attn", "tp"),
        P("attn", "tp"),
        P("tp", "attn"),
        P("attn"),
        P("attn", "tp", None),
        P("attn", "tp"),
        P("tp", "attn"),
        P(None, "tp", None),
        P("tp", None),
        P("attn", None, "tp", None),
        P("attn", "tp", None, None),
        P("tp"),
        P("tp"),
        P("tp"),
        P("tp", None),
        P("attn"),
        P("attn", "tp"),
        P("tp", "attn"),
    )
    out_specs = P(None, None, "attn")
    return jax.shard_map(
        on_device, mesh=mesh, in_specs=in_specs, out_specs=out_specs, check_vma=False
    )
```

```python
import jax
import jax.numpy as jnp
from jax import lax
from jax.experimental import pallas as pl
from jax.experimental.pallas import tpu as pltpu
from jax.sharding import PartitionSpec as P

HEAD_SIZE = 128
EPS = 1e-05
MASKED = -1e30
LANES = 128
STEPS = 2
REQ = 32
ROWS = REQ * STEPS
ATTN = 32
TP = 8
WIDTH = 8192
SLOTS = 64
INNER = 2048
STATES = 256
HEADS = 32
F32 = jnp.float32
BF16 = jnp.bfloat16


def dot(a, b):
    return jnp.dot(a, b, preferred_element_type=F32)


def iota(shape, axis):
    return lax.broadcasted_iota(jnp.int32, shape, axis)


def one_hot(condition):
    return jnp.where(condition, 1.0, 0.0).astype(BF16)


def gain_rows(x, gain):
    squares = jnp.sum(x * x, axis=-1, keepdims=True)
    high = squares.astype(BF16).astype(F32)
    column = iota((x.shape[0], LANES), 1)
    tile = jnp.where(column == 0, high, jnp.where(column == 1, squares - high, 0.0))
    return (x * gain).astype(BF16), tile.astype(BF16)


def scale_of(tile):
    return lax.rsqrt((tile[:, 0:1] + tile[:, 1:2]) / WIDTH + EPS)


def sum_pieces(ref, pieces):
    rows = ref.shape[0] // pieces
    return jnp.sum(ref[...].astype(F32).reshape(pieces, rows, ref.shape[1]), axis=0)


def write_copies(ref, piece, copies):
    piece = piece.astype(ref.dtype)
    for k in range(copies):
        ref[pl.ds(k * piece.shape[0], piece.shape[0]), :] = piece


def slots_by_row(slot_ref, columns):
    request = iota((REQ, columns), 0)
    column = iota((REQ, columns), 1)
    spread = one_hot((column % ROWS) // STEPS == request)
    slots = jnp.broadcast_to(slot_ref[...], (8, REQ)).astype(F32).astype(BF16)
    return dot(slots, spread)[0:1].astype(jnp.int32)


def qkv_kernel(
    hidden, gain, slot_of, lengths, w_key, w_value, w_query, cache,
    out, rows_out, slots_out, lengths_out, cache_out, *scratch
):
    places = (*scratch[:2], slots_out, lengths_out, *scratch[2:5], cache_out)
    copies = []
    for k, source in enumerate((hidden, gain, slot_of, lengths, w_key, w_value, w_query, cache)):
        copies.append(pltpu.make_async_copy(source, places[k], scratch[5].at[k]))
        copies[k].start()
    hidden_here, gain_here, key_here, value_here, query_here = scratch[:5]
    copies[0].wait()
    rows = hidden_here[...].astype(F32).reshape(ROWS, -1)
    rows_out[...] = rows.astype(BF16)
    copies[1].wait()
    normed, tile = gain_rows(rows, gain_here[...])
    for k in range(2, 7):
        copies[k].wait()
    key = dot(normed, key_here[...]).astype(BF16)
    value = dot(normed, value_here[...]).astype(BF16)
    query = dot(normed, query_here[...]).astype(BF16)
    whole = jnp.concatenate([query, key, value, tile], axis=1)
    column = iota((1, ROWS), 1)
    code = slots_by_row(slots_out, ROWS) * 2 + column % STEPS
    chosen = one_hot(iota((2 * SLOTS, ROWS), 0) == code)
    out[...] = dot(chosen, whole).reshape(out.shape).astype(BF16)
    copies[7].wait()


def attend_kernel(pieces, lengths, slot_of, cache, out):
    first_slot = lax.axis_index("attn") * 2
    summed = jnp.sum(pieces[...].astype(F32), axis=0)
    keys_at = 8 * HEAD_SIZE
    columns = keys_at + 2 * HEAD_SIZE
    whole = (summed[:, :columns] * scale_of(summed[:, columns:])).astype(BF16).astype(F32)
    heads = 8
    factor = HEAD_SIZE ** (-0.5)
    group = heads * STEPS
    step_of_row = iota((group, 1), 0) % STEPS
    outputs = []
    for slot in range(2):
        mine = slot_of[...] == first_slot + slot
        length = jnp.sum(jnp.where(mine, lengths[...].astype(F32), 0.0), axis=1, keepdims=True)
        length = length.astype(jnp.int32)
        rows = whole[slot * 2 : slot * 2 + 2]
        query = jnp.concatenate([rows[:, h * LANES : (h + 1) * LANES] for h in range(heads)], axis=0)
        fresh_key = rows[:, keys_at : keys_at + HEAD_SIZE]
        fresh_value = rows[:, keys_at + HEAD_SIZE :]
        scores = (
            lax.dot_general(
                query.astype(BF16), cache[slot, 0], (((1,), (1,)), ((), ())), preferred_element_type=F32
            )
            * factor
        )
        scores = jnp.where(iota(scores.shape, 1) < length, scores, MASKED)
        fresh = []
        for t in range(STEPS):
            score = jnp.sum(query * fresh_key[t : t + 1], axis=-1, keepdims=True) * factor
            fresh.append(jnp.where(step_of_row >= t, score, MASKED))
        top = jnp.maximum(jnp.max(scores, axis=-1, keepdims=True), jnp.maximum(fresh[0], fresh[1]))
        weights = jnp.exp(scores - top)
        total = jnp.sum(weights, axis=-1, keepdims=True)
        mixed = dot(weights.astype(BF16), cache[slot, 1])
        for t in range(STEPS):
            weight = jnp.exp(fresh[t] - top)
            total = total + weight
            mixed = mixed + weight.astype(BF16).astype(F32) * fresh_value[t : t + 1]
        outputs.append(mixed / total)
    halves = []
    for half in range(2):
        for slot in range(2):
            part = outputs[slot]
            first = half * 4
            halves.append(
                jnp.concatenate([part[(first + h) * 2 : (first + h) * 2 + 2] for h in range(4)], axis=1)
            )
    write_copies(out, jnp.concatenate(halves, axis=0), ATTN)


def pair_kernel(own, other, out):
    out[...] = (own[...].astype(F32) + other[...].astype(F32)).astype(BF16)


def sum_chips(own, second, before, after):
    here = own[...].astype(F32) + second[...].astype(F32)
    return here + (before[...].astype(F32) + after[...].astype(F32))


def attn_out_kernel(pieces, slot_of, weight, out):
    column = iota((1, ROWS), 1)
    slots = slots_by_row(slot_of, ROWS) * 4 + column % STEPS
    row = iota((ATTN * 8, ROWS), 0)
    row_code = ((row // 8) * 2 + (row // 2) % 2) * 4 + ((row // 4) % 2) * 2 + row % 2
    gathered = pieces[...]
    total = None
    for half in range(2):
        chosen = one_hot(row_code == slots + half * 2)
        mine = lax.dot_general(chosen, gathered, (((0,), (0,)), ((), ())), preferred_element_type=F32)
        term = dot(mine.astype(BF16), weight[pl.ds(half * 512, 512), :])
        total = term if total is None else total + term
    out[...] = total.astype(BF16)


def mix_in_kernel(own, before, after, second, hidden, gain, w_main, w_step, out, first_out):
    first = (sum_chips(own, second, before, after) + hidden[...].astype(F32)).astype(BF16)
    first_out[...] = first
    normed, tile = gain_rows(first.astype(F32), gain[...])
    main = dot(normed, w_main[...])
    steps = lax.dot_general(
        normed, w_step[...], (((1,), (1,)), ((), ())), preferred_element_type=F32
    )
    both = jnp.concatenate([main, steps, tile[:, : LANES - HEADS].astype(F32)], axis=1)
    out[...] = both.reshape(out.shape).astype(BF16)


def silu(x):
    return x / (1.0 + jnp.exp(-x))


def mamba_kernel(
    pieces, conv_weight, conv_bias, conv_state, state, a_log, dt_bias, skip_gain, group_gain, out
):
    summed = jnp.sum(pieces[...].astype(F32), axis=0)
    state_at = 2 * INNER
    steps_at = state_at + 2 * STATES
    last = summed[:, steps_at:]
    summed = summed * scale_of(last[:, HEADS:])

    def conved(now, cut):
        window = [conv_state[k, :, cut] for k in range(3)] + [now[0:1], now[1:2]]
        totals = []
        for s in range(STEPS):
            total = conv_bias[:, cut]
            for k in range(4):
                total = total + conv_weight[k, :, cut] * window[s + k]
            totals.append(total)
        return silu(jnp.concatenate(totals, axis=0))

    xs = conved(summed[:, INNER:state_at], slice(0, INNER))
    b_in = conved(summed[:, state_at : state_at + STATES], slice(INNER, INNER + STATES))
    c_out = conved(summed[:, state_at + STATES : steps_at], slice(INNER + STATES, INNER + 2 * STATES))
    gate = summed[:, :INNER]
    raw = summed[:, steps_at : steps_at + HEADS] + dt_bias[...]
    step = jnp.maximum(raw, 0.0) + jnp.log1p(jnp.exp(-jnp.abs(raw)))
    decay = jnp.exp(-step * jnp.exp(a_log[...]))
    d0, d1, s0, s1 = decay[0:1], decay[1:2], step[0:1], step[1:2]
    per_head = jnp.concatenate([d0, d0 * d1, s0, d1 * s0, s1, skip_gain[...], d0, d0], axis=0)
    spread = jnp.where(iota((HEADS, INNER), 1) // 64 == iota((HEADS, INNER), 0), 1.0, 0.0)
    wide = jnp.dot(per_head, spread, precision=lax.Precision.HIGHEST, preferred_element_type=F32)
    c_high = c_out.astype(BF16)
    c_low = (c_out - c_high.astype(F32)).astype(BF16)
    whole = state[...]
    high = whole.astype(BF16)
    low = (whole - high.astype(F32)).astype(BF16)
    along = (((1,), (1,)), ((), ()))
    both = jnp.concatenate([c_high, c_low], axis=0)
    by_high = lax.dot_general(both, high, along, preferred_element_type=F32)
    by_low = lax.dot_general(c_high, low, along, preferred_element_type=F32)
    read_old = by_high[0:2] + by_high[2:4] + by_low
    b0c0 = jnp.sum(b_in[0:1] * c_out[0:1], axis=-1, keepdims=True)
    b0c1 = jnp.sum(b_in[0:1] * c_out[1:2], axis=-1, keepdims=True)
    b1c1 = jnp.sum(b_in[1:2] * c_out[1:2], axis=-1, keepdims=True)
    x0, x1 = xs[0:1], xs[1:2]
    read0 = wide[0:1] * read_old[0:1] + wide[2:3] * x0 * b0c0
    read1 = wide[1:2] * read_old[1:2] + wide[3:4] * x0 * b0c1 + wide[4:5] * x1 * b1c1
    read = jnp.concatenate([read0, read1], axis=0) + wide[5:6] * xs
    gated = read * silu(gate)
    mixer = gated * lax.rsqrt(jnp.mean(gated * gated, axis=-1, keepdims=True) + EPS) * group_gain[...]
    piece = jnp.concatenate([mixer[:, q * 512 : (q + 1) * 512] for q in range(4)], axis=0)
    write_copies(out, piece, ATTN)


def project_out_kernel(pieces, weight, out):
    row = iota((4 * ROWS, ATTN * 8), 0)
    column = iota((4 * ROWS, ATTN * 8), 1)
    source = ((row % ROWS) // 2) * 8 + (row // ROWS) * 2 + row % 2
    ordered = dot(one_hot(source == column), pieces[...]).astype(BF16)
    total = None
    for q in range(4):
        term = dot(ordered[q * ROWS : (q + 1) * ROWS], weight[pl.ds(q * 512, 512), :])
        total = term if total is None else total + term
    out[...] = total.astype(BF16)


def up_kernel(own, before, after, opposite, first, gain, w_up, out, second_out):
    second = (sum_chips(own, opposite, before, after) + first[...].astype(F32)).astype(BF16)
    second_out[...] = second
    normed, tile = gain_rows(second.astype(F32), gain[...])
    up = dot(normed, w_up[...])
    both = jnp.concatenate([up, tile.astype(F32)], axis=1)
    out[...] = both.reshape(out.shape).astype(BF16)


def active_kernel(pieces, out):
    summed = jnp.sum(pieces[...].astype(F32), axis=0)
    lifted = jnp.maximum(summed[:, :INNER] * scale_of(summed[:, INNER:]), 0.0)
    active = lifted * lifted
    piece = jnp.concatenate([active[:, q * 512 : (q + 1) * 512] for q in range(4)], axis=0)
    write_copies(out, piece, ATTN)


def last_kernel(own, before, after, opposite, second, out):
    total = sum_chips(own, opposite, before, after) + second[...].astype(F32)
    out[...] = total.reshape(out.shape).astype(BF16)


def call(kernel, outs, *operands, near=False, scratch=(), cost=None):
    space = pltpu.HBM if near else pltpu.VMEM
    shapes = [
        jax.ShapeDtypeStruct(out, BF16) if isinstance(out, tuple) else
        jax.ShapeDtypeStruct(out.shape, out.dtype)
        for out in outs
    ]
    if cost is None:
        cost = sum(x.size * x.dtype.itemsize for x in operands)
    if near:
        operands = [pltpu.with_memory_space_constraint(x, pltpu.HBM) for x in operands]
    result = pl.pallas_call(
        kernel,
        out_shape=shapes,
        in_specs=[pl.BlockSpec(memory_space=space)] * len(operands),
        out_specs=[pl.BlockSpec(memory_space=pltpu.VMEM)] * len(shapes),
        scratch_shapes=scratch,
        cost_estimate=pl.CostEstimate(flops=0, bytes_accessed=cost, transcendentals=0),
        compiler_params=pltpu.CompilerParams(vmem_limit_bytes=24 * 1024 * 1024),
    )(*operands)
    return result[0] if len(shapes) == 1 else result


def exchange(values, axis, pieces):
    rows, columns = values.shape
    cut = values.reshape(pieces, rows // pieces, columns)
    return lax.all_to_all(cut, axis, 0, 0).reshape(rows, columns)


def over_tp(part):
    other = lax.ppermute(part, "tp", [(k, k ^ 1) for k in range(TP)])
    pair = call(pair_kernel, [part.shape], part, other)
    shifted = [lax.ppermute(pair, "tp", [(k, (k + s) % TP) for k in range(TP)]) for s in (4, 2, 6)]
    return [pair, shifted[1], shifted[2], shifted[0]]


def on_device(
    hidden,
    lengths,
    slot_of,
    kv_cache,
    attn_gain,
    w_query,
    key_matrix,
    value_matrix,
    w_attn_out,
    mamba_gain,
    w_mamba_in,
    w_mamba_dt,
    w_mamba_out,
    conv_weight,
    conv_bias,
    conv_state,
    ssm_state,
    a_log,
    dt_bias,
    skip_gain,
    group_gain,
    mlp_gain,
    w_up,
    w_down,
):
    width = hidden.shape[2]
    slot_row = slot_of.reshape(1, REQ)
    owned = ATTN * 8

    def row(x):
        return x.reshape(1, -1)

    length_row = lengths.reshape(1, REQ)
    kept = (hidden, row(attn_gain), key_matrix, value_matrix, w_query)
    pieces, rows, slot_row, length_row, cache = call(
        qkv_kernel, [(ATTN, 4, 1408), (ROWS, width), slot_row, length_row, kv_cache],
        hidden, row(attn_gain), slot_row, length_row, key_matrix, value_matrix, w_query, kv_cache,
        near=True,
        scratch=[pltpu.VMEM(x.shape, x.dtype) for x in kept] + [pltpu.SemaphoreType.DMA((8,))],
        cost=16 * 1024 * 1024,
    )
    pieces = lax.all_to_all(pieces, "attn", 0, 0)
    pieces = call(attend_kernel, [(owned, 512)], pieces, length_row, slot_row, cache)
    pieces = exchange(pieces, "attn", ATTN)
    pieces = call(attn_out_kernel, [(ROWS, width)], pieces, slot_row, w_attn_out)
    pieces = over_tp(pieces)
    pieces, first = call(
        mix_in_kernel, [(ATTN, STEPS, 2 * INNER + 2 * STATES + LANES), (ROWS, width)],
        *pieces, rows, row(mamba_gain), w_mamba_in.reshape(width, -1), w_mamba_dt.T,
    )
    pieces = lax.all_to_all(pieces, "attn", 0, 0)
    pieces = call(
        mamba_kernel, [(owned, 512)],
        pieces, conv_weight, conv_bias, conv_state.reshape(3, 1, -1),
        ssm_state.reshape(INNER, STATES), row(a_log), row(dt_bias), row(skip_gain), group_gain,
    )
    pieces = exchange(pieces, "attn", ATTN)
    pieces = call(project_out_kernel, [(ROWS, width)], pieces, w_mamba_out)
    pieces = over_tp(pieces)
    pieces, second = call(
        up_kernel, [(ATTN, STEPS, INNER + LANES), (ROWS, width)], *pieces, first, row(mlp_gain), w_up
    )
    pieces = lax.all_to_all(pieces, "attn", 0, 0)
    pieces = call(active_kernel, [(owned, 512)], pieces)
    pieces = exchange(pieces, "attn", ATTN)
    pieces = call(project_out_kernel, [(ROWS, width)], pieces, w_down)
    pieces = over_tp(pieces)
    return call(last_kernel, [hidden.shape], *pieces, second)


def solution(mesh):
    in_specs = (
        P(None, None, "attn"),
        P(),
        P(),
        P("attn", None, None, "tp"),
        P("attn"),
        P("attn", "tp"),
        P("attn", "tp"),
        P("attn", "tp"),
        P("tp", "attn"),
        P("attn"),
        P("attn", "tp", None),
        P("attn", "tp"),
        P("tp", "attn"),
        P(None, "tp", None),
        P("tp", None),
        P("attn", None, "tp", None),
        P("attn", "tp", None, None),
        P("tp"),
        P("tp"),
        P("tp"),
        P("tp", None),
        P("attn"),
        P("attn", "tp"),
        P("tp", "attn"),
    )
    out_specs = P(None, None, "attn")
    return jax.shard_map(
        on_device, mesh=mesh, in_specs=in_specs, out_specs=out_specs, check_vma=False
    )
```

```python
import jax
import jax.numpy as jnp
from jax import lax
from jax.experimental import pallas as pl
from jax.experimental.pallas import tpu as pltpu
from jax.sharding import PartitionSpec as P

HEAD_SIZE = 128
EPS = 1e-05
MASKED = -1e30
LANES = 128
STEPS = 2
REQ = 32
ROWS = REQ * STEPS
ATTN = 32
TP = 8
WIDTH = 8192
INNER = 2048
STATES = 256
HEADS = 32
F32 = jnp.float32
BF16 = jnp.bfloat16


def dot(a, b):
    return jnp.dot(a, b, preferred_element_type=F32)


def iota(shape, axis):
    return lax.broadcasted_iota(jnp.int32, shape, axis)


def one_hot(condition):
    return jnp.where(condition, 1.0, 0.0).astype(BF16)


def gain_rows(x, gain):
    squares = jnp.sum(x * x, axis=-1, keepdims=True)
    high = squares.astype(BF16).astype(F32)
    column = iota((x.shape[0], LANES), 1)
    tile = jnp.where(column == 0, high, jnp.where(column == 1, squares - high, 0.0))
    return (x * gain).astype(BF16), tile.astype(BF16)


def scale_of(tile):
    return lax.rsqrt((tile[:, 0:1] + tile[:, 1:2]) / WIDTH + EPS)


def sum_pieces(ref, pieces):
    rows = ref.shape[0] // pieces
    return jnp.sum(ref[...].astype(F32).reshape(pieces, rows, ref.shape[1]), axis=0)


def write_copies(ref, piece, copies):
    piece = piece.astype(ref.dtype)
    for k in range(copies):
        ref[pl.ds(k * piece.shape[0], piece.shape[0]), :] = piece


def slots_by_row(slot_ref, columns):
    request = iota((REQ, columns), 0)
    column = iota((REQ, columns), 1)
    spread = one_hot((column % ROWS) // STEPS == request)
    slots = jnp.broadcast_to(slot_ref[...], (8, REQ)).astype(F32).astype(BF16)
    return dot(slots, spread)[0:1].astype(jnp.int32)


def qkv_kernel(
    hidden, gain, slot_of, lengths, w_key, w_value, w_query, cache,
    out, rows_out, slots_out, lengths_out, cache_out, *scratch
):
    places = (*scratch[:2], slots_out, lengths_out, *scratch[2:5], cache_out)
    copies = []
    for k, source in enumerate((hidden, gain, slot_of, lengths, w_key, w_value, w_query, cache)):
        copies.append(pltpu.make_async_copy(source, places[k], scratch[5].at[k]))
        copies[k].start()
    hidden_here, gain_here, key_here, value_here, query_here = scratch[:5]
    copies[0].wait()
    rows = hidden_here[...].astype(F32).reshape(ROWS, -1)
    rows_out[...] = rows.astype(BF16)
    copies[1].wait()
    normed, tile = gain_rows(rows, gain_here[...])
    for k in range(2, 7):
        copies[k].wait()
    key = dot(normed, key_here[...]).astype(BF16)
    value = dot(normed, value_here[...]).astype(BF16)
    query = dot(normed, query_here[...]).astype(BF16)
    whole = jnp.concatenate([query, key, value, tile], axis=1)
    column = iota((1, ROWS), 1)
    code = slots_by_row(slots_out, ROWS) * 2 + column % STEPS
    row = iota((ROWS, ROWS), 0)
    parts = []
    for slot in range(2):
        chosen = one_hot((row // STEPS) * 4 + slot * 2 + row % STEPS == code)
        parts.append(dot(chosen, whole))
    columns = whole.shape[1] - LANES
    tiles = parts[0][:, columns:] + jnp.concatenate(
        [jnp.zeros((ROWS, 2), F32), parts[1][:, columns : columns + LANES - 2]], axis=1
    )
    both = jnp.concatenate([parts[0][:, :columns], parts[1][:, :columns], tiles], axis=1)
    out[...] = both.reshape(out.shape).astype(BF16)
    copies[7].wait()


def attend_kernel(pieces, lengths, slot_of, cache, out):
    first_slot = lax.axis_index("attn") * 2
    summed = jnp.sum(pieces[...].astype(F32), axis=0)
    keys_at = 8 * HEAD_SIZE
    columns = keys_at + 2 * HEAD_SIZE
    both_rows = []
    for slot in range(2):
        scale = scale_of(summed[:, 2 * columns + 2 * slot :])
        rows = summed[:, slot * columns : (slot + 1) * columns] * scale
        both_rows.append(rows.astype(BF16).astype(F32))
    heads = 8
    factor = HEAD_SIZE ** (-0.5)
    group = heads * STEPS
    step_of_row = iota((group, 1), 0) % STEPS
    queries, kept_rows, all_scores, outputs = [], [], [], []
    for slot in range(2):
        rows = both_rows[slot]
        query = jnp.concatenate([rows[:, h * LANES : (h + 1) * LANES] for h in range(heads)], axis=0)
        queries.append(query)
        kept_rows.append(rows)
        all_scores.append(
            lax.dot_general(
                query.astype(BF16), cache[slot, 0], (((1,), (1,)), ((), ())), preferred_element_type=F32
            )
            * factor
        )
    soft = []
    for slot in range(2):
        mine = slot_of[...] == first_slot + slot
        length = jnp.sum(jnp.where(mine, lengths[...].astype(F32), 0.0), axis=1, keepdims=True)
        length = length.astype(jnp.int32)
        fresh_key = kept_rows[slot][:, keys_at : keys_at + HEAD_SIZE]
        scores = all_scores[slot]
        scores = jnp.where(iota(scores.shape, 1) < length, scores, MASKED)
        fresh = []
        for t in range(STEPS):
            score = jnp.sum(queries[slot] * fresh_key[t : t + 1], axis=-1, keepdims=True) * factor
            fresh.append(jnp.where(step_of_row >= t, score, MASKED))
        top = jnp.maximum(jnp.max(scores, axis=-1, keepdims=True), jnp.maximum(fresh[0], fresh[1]))
        weights = jnp.exp(scores - top)
        total = jnp.sum(weights, axis=-1, keepdims=True)
        soft.append((weights.astype(BF16), total, [jnp.exp(x - top) for x in fresh]))
    for slot in range(2):
        weights, total, fresh = soft[slot]
        fresh_value = kept_rows[slot][:, keys_at + HEAD_SIZE :]
        mixed = dot(weights, cache[slot, 1])
        for t in range(STEPS):
            total = total + fresh[t]
            mixed = mixed + fresh[t].astype(BF16).astype(F32) * fresh_value[t : t + 1]
        outputs.append(mixed / total)
    halves = []
    for half in range(2):
        for slot in range(2):
            part = outputs[slot]
            first = half * 4
            halves.append(
                jnp.concatenate([part[(first + h) * 2 : (first + h) * 2 + 2] for h in range(4)], axis=1)
            )
    write_copies(out, jnp.concatenate(halves, axis=0), ATTN)


def pair_kernel(own, other, out):
    out[...] = (own[...].astype(F32) + other[...].astype(F32)).astype(BF16)


def sum_chips(own, second, before, after):
    here = own[...].astype(F32) + second[...].astype(F32)
    return here + (before[...].astype(F32) + after[...].astype(F32))


def attn_out_kernel(pieces, slot_of, weight, out):
    column = iota((1, ROWS), 1)
    slots = slots_by_row(slot_of, ROWS) * 4 + column % STEPS
    row = iota((ATTN * 8, ROWS), 0)
    row_code = ((row // 8) * 2 + (row // 2) % 2) * 4 + ((row // 4) % 2) * 2 + row % 2
    gathered = pieces[...]
    total = None
    for half in range(2):
        chosen = one_hot(row_code == slots + half * 2)
        mine = lax.dot_general(chosen, gathered, (((0,), (0,)), ((), ())), preferred_element_type=F32)
        term = dot(mine.astype(BF16), weight[pl.ds(half * 512, 512), :])
        total = term if total is None else total + term
    out[...] = total.astype(BF16)


def mix_in_kernel(own, before, after, second, hidden, gain, w_main, w_step, out, first_out):
    first = (sum_chips(own, second, before, after) + hidden[...].astype(F32)).astype(BF16)
    first_out[...] = first
    normed, tile = gain_rows(first.astype(F32), gain[...])
    main = dot(normed, w_main[...])
    steps = lax.dot_general(
        normed, w_step[...], (((1,), (1,)), ((), ())), preferred_element_type=F32
    )
    both = jnp.concatenate([main, steps, tile[:, : LANES - HEADS].astype(F32)], axis=1)
    out[...] = both.reshape(out.shape).astype(BF16)


def silu(x):
    return x / (1.0 + jnp.exp(-x))


def mamba_kernel(
    pieces, conv_weight, conv_bias, conv_state, state, a_log, dt_bias, skip_gain, group_gain, out
):
    summed = jnp.sum(pieces[...].astype(F32), axis=0)
    state_at = 2 * INNER
    steps_at = state_at + 2 * STATES
    last = summed[:, steps_at:]
    summed = summed * scale_of(last[:, HEADS:])

    def conved(now, cut):
        window = [conv_state[k, :, cut] for k in range(3)] + [now[0:1], now[1:2]]
        totals = []
        for s in range(STEPS):
            total = conv_bias[:, cut]
            for k in range(4):
                total = total + conv_weight[k, :, cut] * window[s + k]
            totals.append(total)
        return silu(jnp.concatenate(totals, axis=0))

    xs = conved(summed[:, INNER:state_at], slice(0, INNER))
    b_in = conved(summed[:, state_at : state_at + STATES], slice(INNER, INNER + STATES))
    c_out = conved(summed[:, state_at + STATES : steps_at], slice(INNER + STATES, INNER + 2 * STATES))
    gate = summed[:, :INNER]
    raw = summed[:, steps_at : steps_at + HEADS] + dt_bias[...]
    step = jnp.maximum(raw, 0.0) + jnp.log1p(jnp.exp(-jnp.abs(raw)))
    decay = jnp.exp(-step * jnp.exp(a_log[...]))
    d0, d1, s0, s1 = decay[0:1], decay[1:2], step[0:1], step[1:2]
    per_head = jnp.concatenate([d0, d0 * d1, s0, d1 * s0, s1, skip_gain[...], d0, d0], axis=0)
    spread = one_hot(iota((HEADS, INNER), 1) // 64 == iota((HEADS, INNER), 0))
    wide, rest = None, per_head
    for _ in range(3):
        part = rest.astype(BF16)
        rest = rest - part.astype(F32)
        term = dot(part, spread)
        wide = term if wide is None else wide + term
    c_high = c_out.astype(BF16)
    c_low = (c_out - c_high.astype(F32)).astype(BF16)
    whole = state[...]
    high = whole.astype(BF16)
    low = (whole - high.astype(F32)).astype(BF16)
    along = (((1,), (1,)), ((), ()))
    both = jnp.concatenate([c_high, c_low], axis=0)
    by_high = lax.dot_general(both, high, along, preferred_element_type=F32)
    by_low = lax.dot_general(c_high, low, along, preferred_element_type=F32)
    read_old = by_high[0:2] + by_high[2:4] + by_low
    b0c0 = jnp.sum(b_in[0:1] * c_out[0:1], axis=-1, keepdims=True)
    b0c1 = jnp.sum(b_in[0:1] * c_out[1:2], axis=-1, keepdims=True)
    b1c1 = jnp.sum(b_in[1:2] * c_out[1:2], axis=-1, keepdims=True)
    x0, x1 = xs[0:1], xs[1:2]
    read0 = wide[0:1] * read_old[0:1] + wide[2:3] * x0 * b0c0
    read1 = wide[1:2] * read_old[1:2] + wide[3:4] * x0 * b0c1 + wide[4:5] * x1 * b1c1
    read = jnp.concatenate([read0, read1], axis=0) + wide[5:6] * xs
    gated = read * silu(gate)
    mixer = gated * lax.rsqrt(jnp.mean(gated * gated, axis=-1, keepdims=True) + EPS) * group_gain[...]
    piece = jnp.concatenate([mixer[:, q * 512 : (q + 1) * 512] for q in range(4)], axis=0)
    write_copies(out, piece, ATTN)


def project_out_kernel(pieces, weight, out):
    row = iota((4 * ROWS, ATTN * 8), 0)
    column = iota((4 * ROWS, ATTN * 8), 1)
    source = ((row % ROWS) // 2) * 8 + (row // ROWS) * 2 + row % 2
    ordered = dot(one_hot(source == column), pieces[...]).astype(BF16)
    total = None
    for q in range(4):
        term = dot(ordered[q * ROWS : (q + 1) * ROWS], weight[pl.ds(q * 512, 512), :])
        total = term if total is None else total + term
    out[...] = total.astype(BF16)


def up_kernel(own, before, after, opposite, first, gain, w_up, out, second_out):
    second = (sum_chips(own, opposite, before, after) + first[...].astype(F32)).astype(BF16)
    second_out[...] = second
    normed, tile = gain_rows(second.astype(F32), gain[...])
    up = dot(normed, w_up[...])
    both = jnp.concatenate([up, tile.astype(F32)], axis=1)
    out[...] = both.reshape(out.shape).astype(BF16)


def active_kernel(pieces, out):
    summed = jnp.sum(pieces[...].astype(F32), axis=0)
    lifted = jnp.maximum(summed[:, :INNER] * scale_of(summed[:, INNER:]), 0.0)
    active = lifted * lifted
    piece = jnp.concatenate([active[:, q * 512 : (q + 1) * 512] for q in range(4)], axis=0)
    write_copies(out, piece, ATTN)


def last_kernel(own, before, after, opposite, second, out):
    total = sum_chips(own, opposite, before, after) + second[...].astype(F32)
    out[...] = total.reshape(out.shape).astype(BF16)


def call(kernel, outs, *operands, near=False, scratch=(), cost=None):
    space = pltpu.HBM if near else pltpu.VMEM
    shapes = [
        jax.ShapeDtypeStruct(out, BF16) if isinstance(out, tuple) else
        jax.ShapeDtypeStruct(out.shape, out.dtype)
        for out in outs
    ]
    if cost is None:
        cost = sum(x.size * x.dtype.itemsize for x in operands)
    if near:
        operands = [pltpu.with_memory_space_constraint(x, pltpu.HBM) for x in operands]
    result = pl.pallas_call(
        kernel,
        out_shape=shapes,
        in_specs=[pl.BlockSpec(memory_space=space)] * len(operands),
        out_specs=[pl.BlockSpec(memory_space=pltpu.VMEM)] * len(shapes),
        scratch_shapes=scratch,
        cost_estimate=pl.CostEstimate(flops=0, bytes_accessed=cost, transcendentals=0),
        compiler_params=pltpu.CompilerParams(vmem_limit_bytes=24 * 1024 * 1024),
    )(*operands)
    return result[0] if len(shapes) == 1 else result


def exchange(values, axis, pieces):
    rows, columns = values.shape
    cut = values.reshape(pieces, rows // pieces, columns)
    return lax.all_to_all(cut, axis, 0, 0).reshape(rows, columns)


def over_tp(part):
    other = lax.ppermute(part, "tp", [(k, k ^ 1) for k in range(TP)])
    pair = call(pair_kernel, [part.shape], part, other)
    shifted = [lax.ppermute(pair, "tp", [(k, (k + s) % TP) for k in range(TP)]) for s in (4, 2, 6)]
    return [pair, shifted[1], shifted[2], shifted[0]]


def on_device(
    hidden,
    lengths,
    slot_of,
    kv_cache,
    attn_gain,
    w_query,
    key_matrix,
    value_matrix,
    w_attn_out,
    mamba_gain,
    w_mamba_in,
    w_mamba_dt,
    w_mamba_out,
    conv_weight,
    conv_bias,
    conv_state,
    ssm_state,
    a_log,
    dt_bias,
    skip_gain,
    group_gain,
    mlp_gain,
    w_up,
    w_down,
):
    width = hidden.shape[2]
    slot_row = slot_of.reshape(1, REQ)
    owned = ATTN * 8

    def row(x):
        return x.reshape(1, -1)

    length_row = lengths.reshape(1, REQ)
    kept = (hidden, row(attn_gain), key_matrix, value_matrix, w_query)
    pieces, rows, slot_row, length_row, cache = call(
        qkv_kernel, [(ATTN, STEPS, 2 * 1280 + LANES), (ROWS, width), slot_row, length_row, kv_cache],
        hidden, row(attn_gain), slot_row, length_row, key_matrix, value_matrix, w_query, kv_cache,
        near=True,
        scratch=[pltpu.VMEM(x.shape, x.dtype) for x in kept] + [pltpu.SemaphoreType.DMA((8,))],
        cost=16 * 1024 * 1024,
    )
    pieces = lax.all_to_all(pieces, "attn", 0, 0)
    pieces = call(attend_kernel, [(owned, 512)], pieces, length_row, slot_row, cache)
    pieces = exchange(pieces, "attn", ATTN)
    pieces = call(attn_out_kernel, [(ROWS, width)], pieces, slot_row, w_attn_out)
    pieces = over_tp(pieces)
    pieces, first = call(
        mix_in_kernel, [(ATTN, STEPS, 2 * INNER + 2 * STATES + LANES), (ROWS, width)],
        *pieces, rows, row(mamba_gain), w_mamba_in.reshape(width, -1), w_mamba_dt.T,
    )
    pieces = lax.all_to_all(pieces, "attn", 0, 0)
    pieces = call(
        mamba_kernel, [(owned, 512)],
        pieces, conv_weight, conv_bias, conv_state.reshape(3, 1, -1),
        ssm_state.reshape(INNER, STATES), row(a_log), row(dt_bias), row(skip_gain), group_gain,
    )
    pieces = exchange(pieces, "attn", ATTN)
    pieces = call(project_out_kernel, [(ROWS, width)], pieces, w_mamba_out)
    pieces = over_tp(pieces)
    pieces, second = call(
        up_kernel, [(ATTN, STEPS, INNER + LANES), (ROWS, width)], *pieces, first, row(mlp_gain), w_up
    )
    pieces = lax.all_to_all(pieces, "attn", 0, 0)
    pieces = call(active_kernel, [(owned, 512)], pieces)
    pieces = exchange(pieces, "attn", ATTN)
    pieces = call(project_out_kernel, [(ROWS, width)], pieces, w_down)
    pieces = over_tp(pieces)
    return call(last_kernel, [hidden.shape], *pieces, second)


def solution(mesh):
    in_specs = (
        P(None, None, "attn"),
        P(),
        P(),
        P("attn", None, None, "tp"),
        P("attn"),
        P("attn", "tp"),
        P("attn", "tp"),
        P("attn", "tp"),
        P("tp", "attn"),
        P("attn"),
        P("attn", "tp", None),
        P("attn", "tp"),
        P("tp", "attn"),
        P(None, "tp", None),
        P("tp", None),
        P("attn", None, "tp", None),
        P("attn", "tp", None, None),
        P("tp"),
        P("tp"),
        P("tp"),
        P("tp", None),
        P("attn"),
        P("attn", "tp"),
        P("tp", "attn"),
    )
    out_specs = P(None, None, "attn")
    return jax.shard_map(
        on_device, mesh=mesh, in_specs=in_specs, out_specs=out_specs, check_vma=False
    )
```

```python
import jax
import jax.numpy as jnp
from jax import lax
from jax.experimental import pallas as pl
from jax.experimental.pallas import tpu as pltpu
from jax.sharding import PartitionSpec as P

HEAD_SIZE = 128
EPS = 1e-05
MASKED = -1e30
LANES = 128
STEPS = 2
REQ = 32
ROWS = REQ * STEPS
ATTN = 32
TP = 8
WIDTH = 8192
INNER = 2048
STATES = 256
HEADS = 32
F32 = jnp.float32
BF16 = jnp.bfloat16


def dot(a, b):
    return jnp.dot(a, b, preferred_element_type=F32)


def iota(shape, axis):
    return lax.broadcasted_iota(jnp.int32, shape, axis)


def one_hot(condition):
    return jnp.where(condition, 1.0, 0.0).astype(BF16)


def gain_rows(x, gain):
    squares = jnp.sum(x * x, axis=-1, keepdims=True)
    high = squares.astype(BF16).astype(F32)
    column = iota((x.shape[0], LANES), 1)
    tile = jnp.where(column == 0, high, jnp.where(column == 1, squares - high, 0.0))
    return (x * gain).astype(BF16), tile.astype(BF16)


def scale_of(tile):
    return lax.rsqrt((tile[:, 0:1] + tile[:, 1:2]) / WIDTH + EPS)


def sum_pieces(ref, pieces):
    rows = ref.shape[0] // pieces
    return jnp.sum(ref[...].astype(F32).reshape(pieces, rows, ref.shape[1]), axis=0)


def write_copies(ref, piece, copies):
    piece = piece.astype(ref.dtype)
    for k in range(copies):
        ref[pl.ds(k * piece.shape[0], piece.shape[0]), :] = piece


def slots_by_row(slot_ref, columns):
    request = iota((REQ, columns), 0)
    column = iota((REQ, columns), 1)
    spread = one_hot((column % ROWS) // STEPS == request)
    slots = jnp.broadcast_to(slot_ref[...], (8, REQ)).astype(F32).astype(BF16)
    return dot(slots, spread)[0:1].astype(jnp.int32)


def qkv_kernel(
    hidden, gain, slot_of, lengths, w_key, w_value, w_query, cache,
    out, rows_out, slots_out, lengths_out, cache_out, *scratch
):
    places = (*scratch[:2], slots_out, lengths_out, *scratch[2:5], cache_out)
    copies = []
    for k, source in enumerate((hidden, gain, slot_of, lengths, w_key, w_value, w_query, cache)):
        copies.append(pltpu.make_async_copy(source, places[k], scratch[5].at[k]))
        copies[k].start()
    hidden_here, gain_here, key_here, value_here, query_here = scratch[:5]
    copies[0].wait()
    rows = hidden_here[...].astype(F32).reshape(ROWS, -1)
    rows_out[...] = rows.astype(BF16)
    copies[1].wait()
    normed, tile = gain_rows(rows, gain_here[...])
    for k in range(2, 7):
        copies[k].wait()
    key = dot(normed, key_here[...]).astype(BF16)
    value = dot(normed, value_here[...]).astype(BF16)
    query = dot(normed, query_here[...]).astype(BF16)
    whole = jnp.concatenate([query, key, value, tile], axis=1)
    column = iota((1, ROWS), 1)
    code = slots_by_row(slots_out, ROWS) * 2 + column % STEPS
    row = iota((ROWS, ROWS), 0)
    parts = []
    for slot in range(2):
        chosen = one_hot((row // STEPS) * 4 + slot * 2 + row % STEPS == code)
        parts.append(dot(chosen, whole))
    columns = whole.shape[1] - LANES
    tiles = parts[0][:, columns:] + jnp.concatenate(
        [jnp.zeros((ROWS, 2), F32), parts[1][:, columns : columns + LANES - 2]], axis=1
    )
    both = jnp.concatenate([parts[0][:, :columns], parts[1][:, :columns], tiles], axis=1)
    out[...] = both.reshape(out.shape).astype(BF16)
    copies[7].wait()


def attend_kernel(pieces, lengths, slot_of, cache, out):
    first_slot = lax.axis_index("attn") * 2
    summed = jnp.sum(pieces[...].astype(F32), axis=0)
    keys_at = 8 * HEAD_SIZE
    columns = keys_at + 2 * HEAD_SIZE
    both_rows = []
    for slot in range(2):
        scale = scale_of(summed[:, 2 * columns + 2 * slot :])
        rows = summed[:, slot * columns : (slot + 1) * columns] * scale
        both_rows.append(rows.astype(BF16).astype(F32))
    heads = 8
    factor = HEAD_SIZE ** (-0.5)
    group = heads * STEPS
    step_of_row = iota((group, 1), 0) % STEPS
    queries, kept_rows, all_scores, outputs = [], [], [], []
    for slot in range(2):
        rows = both_rows[slot]
        query = jnp.concatenate([rows[:, h * LANES : (h + 1) * LANES] for h in range(heads)], axis=0)
        queries.append(query)
        kept_rows.append(rows)
        all_scores.append(
            lax.dot_general(
                query.astype(BF16), cache[slot, 0], (((1,), (1,)), ((), ())), preferred_element_type=F32
            )
            * factor
        )
    soft = []
    for slot in range(2):
        mine = slot_of[...] == first_slot + slot
        length = jnp.sum(jnp.where(mine, lengths[...].astype(F32), 0.0), axis=1, keepdims=True)
        length = length.astype(jnp.int32)
        fresh_key = kept_rows[slot][:, keys_at : keys_at + HEAD_SIZE]
        scores = all_scores[slot]
        scores = jnp.where(iota(scores.shape, 1) < length, scores, MASKED)
        fresh = []
        for t in range(STEPS):
            score = jnp.sum(queries[slot] * fresh_key[t : t + 1], axis=-1, keepdims=True) * factor
            fresh.append(jnp.where(step_of_row >= t, score, MASKED))
        top = jnp.maximum(jnp.max(scores, axis=-1, keepdims=True), jnp.maximum(fresh[0], fresh[1]))
        weights = jnp.exp(scores - top)
        total = jnp.sum(weights, axis=-1, keepdims=True)
        soft.append((weights.astype(BF16), total, [jnp.exp(x - top) for x in fresh]))
    for slot in range(2):
        weights, total, fresh = soft[slot]
        fresh_value = kept_rows[slot][:, keys_at + HEAD_SIZE :]
        mixed = dot(weights, cache[slot, 1])
        for t in range(STEPS):
            total = total + fresh[t]
            mixed = mixed + fresh[t].astype(BF16).astype(F32) * fresh_value[t : t + 1]
        outputs.append(mixed / total)
    halves = []
    for half in range(2):
        for slot in range(2):
            part = outputs[slot]
            first = half * 4
            halves.append(
                jnp.concatenate([part[(first + h) * 2 : (first + h) * 2 + 2] for h in range(4)], axis=1)
            )
    write_copies(out, jnp.concatenate(halves, axis=0), ATTN)


def pair_kernel(own, other, out):
    out[...] = (own[...].astype(F32) + other[...].astype(F32)).astype(BF16)


def sum_chips(own, second, before, after):
    here = own[...].astype(F32) + second[...].astype(F32)
    return here + (before[...].astype(F32) + after[...].astype(F32))


def attn_out_kernel(pieces, slot_of, weight, out):
    column = iota((1, ROWS), 1)
    slots = slots_by_row(slot_of, ROWS) * 4 + column % STEPS
    row = iota((ATTN * 8, ROWS), 0)
    row_code = ((row // 8) * 2 + (row // 2) % 2) * 4 + ((row // 4) % 2) * 2 + row % 2
    gathered = pieces[...]
    total = None
    for half in range(2):
        chosen = one_hot(row_code == slots + half * 2)
        mine = lax.dot_general(chosen, gathered, (((0,), (0,)), ((), ())), preferred_element_type=F32)
        term = dot(mine.astype(BF16), weight[pl.ds(half * 512, 512), :])
        total = term if total is None else total + term
    out[...] = total.astype(BF16)


def mix_in_kernel(own, before, after, second, hidden, gain, w_main, w_step, out, first_out):
    first = (sum_chips(own, second, before, after) + hidden[...].astype(F32)).astype(BF16)
    first_out[...] = first
    normed, tile = gain_rows(first.astype(F32), gain[...])
    main = dot(normed, w_main[...])
    steps = lax.dot_general(
        normed, w_step[...], (((1,), (1,)), ((), ())), preferred_element_type=F32
    )
    both = jnp.concatenate([main, steps, tile[:, : LANES - HEADS].astype(F32)], axis=1)
    out[...] = both.reshape(out.shape).astype(BF16)


def silu(x):
    return x / (1.0 + jnp.exp(-x))


def mamba_kernel(
    pieces, conv_weight, conv_bias, conv_state, state, a_log, dt_bias, skip_gain, group_gain, out
):
    summed = jnp.sum(pieces[...].astype(F32), axis=0)
    state_at = 2 * INNER
    steps_at = state_at + 2 * STATES
    last = summed[:, steps_at:]
    summed = summed * scale_of(last[:, HEADS:])

    def conved(now, cut):
        window = [conv_state[k, :, cut] for k in range(3)] + [now[0:1], now[1:2]]
        totals = []
        for s in range(STEPS):
            total = conv_bias[:, cut]
            for k in range(4):
                total = total + conv_weight[k, :, cut] * window[s + k]
            totals.append(total)
        return silu(jnp.concatenate(totals, axis=0))

    xs = conved(summed[:, INNER:state_at], slice(0, INNER))
    b_in = conved(summed[:, state_at : state_at + STATES], slice(INNER, INNER + STATES))
    c_out = conved(summed[:, state_at + STATES : steps_at], slice(INNER + STATES, INNER + 2 * STATES))
    gate = summed[:, :INNER]
    raw = summed[:, steps_at : steps_at + HEADS] + dt_bias[...]
    step = jnp.maximum(raw, 0.0) + jnp.log1p(jnp.exp(-jnp.abs(raw)))
    decay = jnp.exp(-step * jnp.exp(a_log[...]))
    d0, d1, s0, s1 = decay[0:1], decay[1:2], step[0:1], step[1:2]
    per_head = jnp.concatenate([d0, d0 * d1, s0, d1 * s0, s1, skip_gain[...], d0, d0], axis=0)
    spread = one_hot(iota((HEADS, INNER), 1) // 64 == iota((HEADS, INNER), 0))
    wide, rest = None, per_head
    for _ in range(3):
        part = rest.astype(BF16)
        rest = rest - part.astype(F32)
        term = dot(part, spread)
        wide = term if wide is None else wide + term
    c_high = c_out.astype(BF16)
    c_low = (c_out - c_high.astype(F32)).astype(BF16)
    whole = state[...]
    high = whole.astype(BF16)
    low = (whole - high.astype(F32)).astype(BF16)
    along = (((1,), (1,)), ((), ()))
    both = jnp.concatenate([c_high, c_low], axis=0)
    by_high = lax.dot_general(both, high, along, preferred_element_type=F32)
    by_low = lax.dot_general(c_high, low, along, preferred_element_type=F32)
    read_old = by_high[0:2] + by_high[2:4] + by_low
    b0c0 = jnp.sum(b_in[0:1] * c_out[0:1], axis=-1, keepdims=True)
    b0c1 = jnp.sum(b_in[0:1] * c_out[1:2], axis=-1, keepdims=True)
    b1c1 = jnp.sum(b_in[1:2] * c_out[1:2], axis=-1, keepdims=True)
    x0, x1 = xs[0:1], xs[1:2]
    read0 = wide[0:1] * read_old[0:1] + wide[2:3] * x0 * b0c0
    read1 = wide[1:2] * read_old[1:2] + wide[3:4] * x0 * b0c1 + wide[4:5] * x1 * b1c1
    read = jnp.concatenate([read0, read1], axis=0) + wide[5:6] * xs
    gated = read * silu(gate)
    mixer = gated * lax.rsqrt(jnp.mean(gated * gated, axis=-1, keepdims=True) + EPS) * group_gain[...]
    piece = jnp.concatenate([mixer[:, q * 512 : (q + 1) * 512] for q in range(4)], axis=0)
    write_copies(out, piece, ATTN)


def project_out_kernel(pieces, weight, out):
    row = iota((4 * ROWS, ATTN * 8), 0)
    column = iota((4 * ROWS, ATTN * 8), 1)
    source = ((row % ROWS) // 2) * 8 + (row // ROWS) * 2 + row % 2
    ordered = dot(one_hot(source == column), pieces[...]).astype(BF16)
    total = None
    for q in range(4):
        term = dot(ordered[q * ROWS : (q + 1) * ROWS], weight[pl.ds(q * 512, 512), :])
        total = term if total is None else total + term
    out[...] = total.astype(BF16)


def up_kernel(own, before, after, opposite, first, gain, w_up, out, second_out):
    second = (sum_chips(own, opposite, before, after) + first[...].astype(F32)).astype(BF16)
    second_out[...] = second
    normed, tile = gain_rows(second.astype(F32), gain[...])
    up = dot(normed, w_up[...])
    both = jnp.concatenate([up, tile.astype(F32)], axis=1)
    out[...] = both.reshape(out.shape).astype(BF16)


def active_kernel(pieces, out):
    summed = jnp.sum(pieces[...].astype(F32), axis=0)
    lifted = jnp.maximum(summed[:, :INNER] * scale_of(summed[:, INNER:]), 0.0)
    active = lifted * lifted
    piece = jnp.concatenate([active[:, q * 512 : (q + 1) * 512] for q in range(4)], axis=0)
    write_copies(out, piece, ATTN)


def last_kernel(own, before, after, opposite, second, out):
    total = sum_chips(own, opposite, before, after) + second[...].astype(F32)
    out[...] = total.reshape(out.shape).astype(BF16)


def call(kernel, outs, *operands, near=False, scratch=(), cost=None):
    space = pltpu.HBM if near else pltpu.VMEM
    shapes = [
        jax.ShapeDtypeStruct(out, BF16) if isinstance(out, tuple) else
        jax.ShapeDtypeStruct(out.shape, out.dtype)
        for out in outs
    ]
    if cost is None:
        cost = sum(x.size * x.dtype.itemsize for x in operands)
    if near:
        operands = [pltpu.with_memory_space_constraint(x, pltpu.HBM) for x in operands]
    result = pl.pallas_call(
        kernel,
        out_shape=shapes,
        in_specs=[pl.BlockSpec(memory_space=space)] * len(operands),
        out_specs=[pl.BlockSpec(memory_space=pltpu.VMEM)] * len(shapes),
        scratch_shapes=scratch,
        cost_estimate=pl.CostEstimate(flops=0, bytes_accessed=cost, transcendentals=0),
        compiler_params=pltpu.CompilerParams(vmem_limit_bytes=24 * 1024 * 1024),
    )(*operands)
    return result[0] if len(shapes) == 1 else result


def exchange(values, axis, pieces):
    rows, columns = values.shape
    cut = values.reshape(pieces, rows // pieces, columns)
    return lax.all_to_all(cut, axis, 0, 0).reshape(rows, columns)


def over_tp(part):
    other = lax.ppermute(part, "tp", [(k, k ^ 1) for k in range(TP)])
    pair = call(pair_kernel, [part.shape], part, other)
    shifted = [lax.ppermute(pair, "tp", [(k, k ^ s) for k in range(TP)]) for s in (4, 2, 6)]
    return [pair, shifted[1], shifted[2], shifted[0]]


def on_device(
    hidden,
    lengths,
    slot_of,
    kv_cache,
    attn_gain,
    w_query,
    key_matrix,
    value_matrix,
    w_attn_out,
    mamba_gain,
    w_mamba_in,
    w_mamba_dt,
    w_mamba_out,
    conv_weight,
    conv_bias,
    conv_state,
    ssm_state,
    a_log,
    dt_bias,
    skip_gain,
    group_gain,
    mlp_gain,
    w_up,
    w_down,
):
    width = hidden.shape[2]
    slot_row = slot_of.reshape(1, REQ)
    owned = ATTN * 8

    def row(x):
        return x.reshape(1, -1)

    length_row = lengths.reshape(1, REQ)
    kept = (hidden, row(attn_gain), key_matrix, value_matrix, w_query)
    pieces, rows, slot_row, length_row, cache = call(
        qkv_kernel, [(ATTN, STEPS, 2 * 1280 + LANES), (ROWS, width), slot_row, length_row, kv_cache],
        hidden, row(attn_gain), slot_row, length_row, key_matrix, value_matrix, w_query, kv_cache,
        near=True,
        scratch=[pltpu.VMEM(x.shape, x.dtype) for x in kept] + [pltpu.SemaphoreType.DMA((8,))],
        cost=16 * 1024 * 1024,
    )
    pieces = lax.all_to_all(pieces, "attn", 0, 0)
    pieces = call(attend_kernel, [(owned, 512)], pieces, length_row, slot_row, cache)
    pieces = exchange(pieces, "attn", ATTN)
    pieces = call(attn_out_kernel, [(ROWS, width)], pieces, slot_row, w_attn_out)
    pieces = over_tp(pieces)
    pieces, first = call(
        mix_in_kernel, [(ATTN, STEPS, 2 * INNER + 2 * STATES + LANES), (ROWS, width)],
        *pieces, rows, row(mamba_gain), w_mamba_in.reshape(width, -1), w_mamba_dt.T,
    )
    pieces = lax.all_to_all(pieces, "attn", 0, 0)
    pieces = call(
        mamba_kernel, [(owned, 512)],
        pieces, conv_weight, conv_bias, conv_state.reshape(3, 1, -1),
        ssm_state.reshape(INNER, STATES), row(a_log), row(dt_bias), row(skip_gain), group_gain,
    )
    pieces = exchange(pieces, "attn", ATTN)
    pieces = call(project_out_kernel, [(ROWS, width)], pieces, w_mamba_out)
    pieces = over_tp(pieces)
    pieces, second = call(
        up_kernel, [(ATTN, STEPS, INNER + LANES), (ROWS, width)], *pieces, first, row(mlp_gain), w_up
    )
    pieces = lax.all_to_all(pieces, "attn", 0, 0)
    pieces = call(active_kernel, [(owned, 512)], pieces)
    pieces = exchange(pieces, "attn", ATTN)
    pieces = call(project_out_kernel, [(ROWS, width)], pieces, w_down)
    pieces = over_tp(pieces)
    return call(last_kernel, [hidden.shape], *pieces, second)


def solution(mesh):
    in_specs = (
        P(None, None, "attn"),
        P(),
        P(),
        P("attn", None, None, "tp"),
        P("attn"),
        P("attn", "tp"),
        P("attn", "tp"),
        P("attn", "tp"),
        P("tp", "attn"),
        P("attn"),
        P("attn", "tp", None),
        P("attn", "tp"),
        P("tp", "attn"),
        P(None, "tp", None),
        P("tp", None),
        P("attn", None, "tp", None),
        P("attn", "tp", None, None),
        P("tp"),
        P("tp"),
        P("tp"),
        P("tp", None),
        P("attn"),
        P("attn", "tp"),
        P("tp", "attn"),
    )
    out_specs = P(None, None, "attn")
    return jax.shard_map(
        on_device, mesh=mesh, in_specs=in_specs, out_specs=out_specs, check_vma=False
    )
```

```python
import jax
import jax.numpy as jnp
from jax import lax
from jax.experimental import pallas as pl
from jax.experimental.pallas import tpu as pltpu
from jax.sharding import PartitionSpec as P

HEAD_SIZE = 128
EPS = 1e-05
MASKED = -1e30
LANES = 128
STEPS = 2
REQ = 32
ROWS = REQ * STEPS
ATTN = 32
TP = 8
WIDTH = 8192
INNER = 2048
STATES = 256
HEADS = 32
F32 = jnp.float32
BF16 = jnp.bfloat16


def dot(a, b):
    return jnp.dot(a, b, preferred_element_type=F32)


def iota(shape, axis):
    return lax.broadcasted_iota(jnp.int32, shape, axis)


def one_hot(condition):
    return jnp.where(condition, 1.0, 0.0).astype(BF16)


def gain_rows(x, gain):
    squares = jnp.sum(x * x, axis=-1, keepdims=True)
    high = squares.astype(BF16).astype(F32)
    column = iota((x.shape[0], LANES), 1)
    tile = jnp.where(column == 0, high, jnp.where(column == 1, squares - high, 0.0))
    return (x * gain).astype(BF16), tile.astype(BF16)


def scale_of(tile):
    return lax.rsqrt((tile[:, 0:1] + tile[:, 1:2]) / WIDTH + EPS)


def sum_pieces(ref, pieces):
    rows = ref.shape[0] // pieces
    return jnp.sum(ref[...].astype(F32).reshape(pieces, rows, ref.shape[1]), axis=0)


def sum_by_step(ref):
    devices, steps, columns = ref.shape
    rows = ref[...].reshape(devices * steps, columns)
    row, source = iota((8, devices * steps), 0), iota((8, devices * steps), 1)
    return dot(one_hot(source % steps == row), rows)[:steps]


def write_copies(ref, piece, copies):
    piece = piece.astype(ref.dtype)
    for k in range(copies):
        ref[pl.ds(k * piece.shape[0], piece.shape[0]), :] = piece


def slots_by_row(slot_ref, columns):
    request = iota((REQ, columns), 0)
    column = iota((REQ, columns), 1)
    spread = one_hot((column % ROWS) // STEPS == request)
    slots = jnp.broadcast_to(slot_ref[...], (8, REQ)).astype(F32).astype(BF16)
    return dot(slots, spread)[0:1].astype(jnp.int32)


def qkv_kernel(
    hidden, gain, slot_of, lengths, w_key, w_value, w_query, cache,
    out, rows_out, slots_out, lengths_out, cache_out, *scratch
):
    places = (*scratch[:2], slots_out, lengths_out, *scratch[2:5], cache_out)
    copies = []
    for k, source in enumerate((hidden, gain, slot_of, lengths, w_key, w_value, w_query, cache)):
        copies.append(pltpu.make_async_copy(source, places[k], scratch[5].at[k]))
        copies[k].start()
    hidden_here, gain_here, key_here, value_here, query_here = scratch[:5]
    copies[0].wait()
    rows = hidden_here[...].astype(F32).reshape(ROWS, -1)
    rows_out[...] = rows.astype(BF16)
    copies[1].wait()
    normed, tile = gain_rows(rows, gain_here[...])
    for k in range(2, 7):
        copies[k].wait()
    key = dot(normed, key_here[...]).astype(BF16)
    value = dot(normed, value_here[...]).astype(BF16)
    query = dot(normed, query_here[...]).astype(BF16)
    whole = jnp.concatenate([query, key, value, tile], axis=1)
    column = iota((1, ROWS), 1)
    code = slots_by_row(slots_out, ROWS) * 2 + column % STEPS
    row = iota((ROWS, ROWS), 0)
    parts = []
    for slot in range(2):
        chosen = one_hot((row // STEPS) * 4 + slot * 2 + row % STEPS == code)
        parts.append(dot(chosen, whole))
    columns = whole.shape[1] - LANES
    tiles = parts[0][:, columns:] + jnp.concatenate(
        [jnp.zeros((ROWS, 2), F32), parts[1][:, columns : columns + LANES - 2]], axis=1
    )
    both = jnp.concatenate([parts[0][:, :columns], parts[1][:, :columns], tiles], axis=1)
    out[...] = both.reshape(out.shape).astype(BF16)
    copies[7].wait()


def attend_kernel(pieces, lengths, slot_of, cache, out):
    first_slot = lax.axis_index("attn") * 2
    summed = sum_by_step(pieces)
    keys_at = 8 * HEAD_SIZE
    columns = keys_at + 2 * HEAD_SIZE
    both_rows = []
    for slot in range(2):
        scale = scale_of(summed[:, 2 * columns + 2 * slot :])
        rows = summed[:, slot * columns : (slot + 1) * columns] * scale
        both_rows.append(rows.astype(BF16).astype(F32))
    heads = 8
    factor = HEAD_SIZE ** (-0.5)
    group = heads * STEPS
    step_of_row = iota((group, 1), 0) % STEPS
    queries, kept_rows, all_scores, outputs = [], [], [], []
    for slot in range(2):
        rows = both_rows[slot]
        query = jnp.concatenate([rows[:, h * LANES : (h + 1) * LANES] for h in range(heads)], axis=0)
        queries.append(query)
        kept_rows.append(rows)
        all_scores.append(
            lax.dot_general(
                query.astype(BF16), cache[slot, 0], (((1,), (1,)), ((), ())), preferred_element_type=F32
            )
            * factor
        )
    soft = []
    for slot in range(2):
        mine = slot_of[...] == first_slot + slot
        length = jnp.sum(jnp.where(mine, lengths[...].astype(F32), 0.0), axis=1, keepdims=True)
        length = length.astype(jnp.int32)
        fresh_key = kept_rows[slot][:, keys_at : keys_at + HEAD_SIZE]
        scores = all_scores[slot]
        scores = jnp.where(iota(scores.shape, 1) < length, scores, MASKED)
        fresh = []
        for t in range(STEPS):
            score = jnp.sum(queries[slot] * fresh_key[t : t + 1], axis=-1, keepdims=True) * factor
            fresh.append(jnp.where(step_of_row >= t, score, MASKED))
        top = jnp.maximum(jnp.max(scores, axis=-1, keepdims=True), jnp.maximum(fresh[0], fresh[1]))
        weights = jnp.exp(scores - top)
        total = jnp.sum(weights, axis=-1, keepdims=True)
        soft.append((weights.astype(BF16), total, [jnp.exp(x - top) for x in fresh]))
    for slot in range(2):
        weights, total, fresh = soft[slot]
        fresh_value = kept_rows[slot][:, keys_at + HEAD_SIZE :]
        mixed = dot(weights, cache[slot, 1])
        for t in range(STEPS):
            total = total + fresh[t]
            mixed = mixed + fresh[t].astype(BF16).astype(F32) * fresh_value[t : t + 1]
        outputs.append(mixed / total)
    halves = []
    for half in range(2):
        for slot in range(2):
            part = outputs[slot]
            first = half * 4
            halves.append(
                jnp.concatenate([part[(first + h) * 2 : (first + h) * 2 + 2] for h in range(4)], axis=1)
            )
    write_copies(out, jnp.concatenate(halves, axis=0), ATTN)


def pair_kernel(own, other, out):
    out[...] = (own[...].astype(F32) + other[...].astype(F32)).astype(BF16)


def sum_chips(own, second, before, after):
    here = own[...].astype(F32) + second[...].astype(F32)
    return here + (before[...].astype(F32) + after[...].astype(F32))


def attn_out_kernel(pieces, slot_of, weight, out):
    column = iota((1, ROWS), 1)
    slots = slots_by_row(slot_of, ROWS) * 4 + column % STEPS
    row = iota((ATTN * 8, ROWS), 0)
    row_code = ((row // 8) * 2 + (row // 2) % 2) * 4 + ((row // 4) % 2) * 2 + row % 2
    gathered = pieces[...]
    total = None
    for half in range(2):
        chosen = one_hot(row_code == slots + half * 2)
        mine = lax.dot_general(chosen, gathered, (((0,), (0,)), ((), ())), preferred_element_type=F32)
        term = dot(mine.astype(BF16), weight[pl.ds(half * 512, 512), :])
        total = term if total is None else total + term
    out[...] = total.astype(BF16)


def mix_in_kernel(own, before, after, second, hidden, gain, w_main, w_step, out, first_out):
    first = (sum_chips(own, second, before, after) + hidden[...].astype(F32)).astype(BF16)
    first_out[...] = first
    normed, tile = gain_rows(first.astype(F32), gain[...])
    main = dot(normed, w_main[...])
    steps = lax.dot_general(
        normed, w_step[...], (((1,), (1,)), ((), ())), preferred_element_type=F32
    )
    both = jnp.concatenate([main, steps, tile[:, : LANES - HEADS].astype(F32)], axis=1)
    out[...] = both.reshape(out.shape).astype(BF16)


def silu(x):
    return x / (1.0 + jnp.exp(-x))


def mamba_kernel(
    pieces, conv_weight, conv_bias, conv_state, state, a_log, dt_bias, skip_gain, group_gain, out
):
    summed = sum_by_step(pieces)
    state_at = 2 * INNER
    steps_at = state_at + 2 * STATES
    last = summed[:, steps_at:]
    summed = summed * scale_of(last[:, HEADS:])

    def conved(now, cut):
        window = [conv_state[k, :, cut] for k in range(3)] + [now[0:1], now[1:2]]
        totals = []
        for s in range(STEPS):
            total = conv_bias[:, cut]
            for k in range(4):
                total = total + conv_weight[k, :, cut] * window[s + k]
            totals.append(total)
        return silu(jnp.concatenate(totals, axis=0))

    xs = conved(summed[:, INNER:state_at], slice(0, INNER))
    b_in = conved(summed[:, state_at : state_at + STATES], slice(INNER, INNER + STATES))
    c_out = conved(summed[:, state_at + STATES : steps_at], slice(INNER + STATES, INNER + 2 * STATES))
    gate = summed[:, :INNER]
    raw = summed[:, steps_at : steps_at + HEADS] + dt_bias[...]
    step = jnp.maximum(raw, 0.0) + jnp.log1p(jnp.exp(-jnp.abs(raw)))
    decay = jnp.exp(-step * jnp.exp(a_log[...]))
    d0, d1, s0, s1 = decay[0:1], decay[1:2], step[0:1], step[1:2]
    per_head = jnp.concatenate([d0, d0 * d1, s0, d1 * s0, s1, skip_gain[...], d0, d0], axis=0)
    spread = one_hot(iota((HEADS, INNER), 1) // 64 == iota((HEADS, INNER), 0))
    wide, rest = None, per_head
    for _ in range(3):
        part = rest.astype(BF16)
        rest = rest - part.astype(F32)
        term = dot(part, spread)
        wide = term if wide is None else wide + term
    c_high = c_out.astype(BF16)
    c_low = (c_out - c_high.astype(F32)).astype(BF16)
    whole = state[...]
    high = whole.astype(BF16)
    low = (whole - high.astype(F32)).astype(BF16)
    along = (((1,), (1,)), ((), ()))
    both = jnp.concatenate([c_high, c_low], axis=0)
    by_high = lax.dot_general(both, high, along, preferred_element_type=F32)
    by_low = lax.dot_general(c_high, low, along, preferred_element_type=F32)
    read_old = by_high[0:2] + by_high[2:4] + by_low
    b0c0 = jnp.sum(b_in[0:1] * c_out[0:1], axis=-1, keepdims=True)
    b0c1 = jnp.sum(b_in[0:1] * c_out[1:2], axis=-1, keepdims=True)
    b1c1 = jnp.sum(b_in[1:2] * c_out[1:2], axis=-1, keepdims=True)
    x0, x1 = xs[0:1], xs[1:2]
    read0 = wide[0:1] * read_old[0:1] + wide[2:3] * x0 * b0c0
    read1 = wide[1:2] * read_old[1:2] + wide[3:4] * x0 * b0c1 + wide[4:5] * x1 * b1c1
    read = jnp.concatenate([read0, read1], axis=0) + wide[5:6] * xs
    gated = read * silu(gate)
    mixer = gated * lax.rsqrt(jnp.mean(gated * gated, axis=-1, keepdims=True) + EPS) * group_gain[...]
    piece = jnp.concatenate([mixer[:, q * 512 : (q + 1) * 512] for q in range(4)], axis=0)
    write_copies(out, piece, ATTN)


def project_out_kernel(pieces, weight, out):
    row = iota((4 * ROWS, ATTN * 8), 0)
    column = iota((4 * ROWS, ATTN * 8), 1)
    source = ((row % ROWS) // 2) * 8 + (row // ROWS) * 2 + row % 2
    ordered = dot(one_hot(source == column), pieces[...]).astype(BF16)
    total = None
    for q in range(4):
        term = dot(ordered[q * ROWS : (q + 1) * ROWS], weight[pl.ds(q * 512, 512), :])
        total = term if total is None else total + term
    out[...] = total.astype(BF16)


def up_kernel(own, before, after, opposite, first, gain, w_up, out, second_out):
    second = (sum_chips(own, opposite, before, after) + first[...].astype(F32)).astype(BF16)
    second_out[...] = second
    normed, tile = gain_rows(second.astype(F32), gain[...])
    up = dot(normed, w_up[...])
    both = jnp.concatenate([up, tile.astype(F32)], axis=1)
    out[...] = both.reshape(out.shape).astype(BF16)


def active_kernel(pieces, out):
    summed = sum_by_step(pieces)
    lifted = jnp.maximum(summed[:, :INNER] * scale_of(summed[:, INNER:]), 0.0)
    active = lifted * lifted
    piece = jnp.concatenate([active[:, q * 512 : (q + 1) * 512] for q in range(4)], axis=0)
    write_copies(out, piece, ATTN)


def last_kernel(own, before, after, opposite, second, out):
    total = sum_chips(own, opposite, before, after) + second[...].astype(F32)
    out[...] = total.reshape(out.shape).astype(BF16)


def call(kernel, outs, *operands, near=False, scratch=(), cost=None):
    space = pltpu.HBM if near else pltpu.VMEM
    shapes = [
        jax.ShapeDtypeStruct(out, BF16) if isinstance(out, tuple) else
        jax.ShapeDtypeStruct(out.shape, out.dtype)
        for out in outs
    ]
    if cost is None:
        cost = sum(x.size * x.dtype.itemsize for x in operands)
    if near:
        operands = [pltpu.with_memory_space_constraint(x, pltpu.HBM) for x in operands]
    result = pl.pallas_call(
        kernel,
        out_shape=shapes,
        in_specs=[pl.BlockSpec(memory_space=space)] * len(operands),
        out_specs=[pl.BlockSpec(memory_space=pltpu.VMEM)] * len(shapes),
        scratch_shapes=scratch,
        cost_estimate=pl.CostEstimate(flops=0, bytes_accessed=cost, transcendentals=0),
        compiler_params=pltpu.CompilerParams(vmem_limit_bytes=24 * 1024 * 1024),
    )(*operands)
    return result[0] if len(shapes) == 1 else result


def exchange(values, axis, pieces):
    rows, columns = values.shape
    cut = values.reshape(pieces, rows // pieces, columns)
    return lax.all_to_all(cut, axis, 0, 0).reshape(rows, columns)


def over_tp(part):
    other = lax.ppermute(part, "tp", [(k, k ^ 1) for k in range(TP)])
    pair = call(pair_kernel, [part.shape], part, other)
    shifted = [lax.ppermute(pair, "tp", [(k, k ^ s) for k in range(TP)]) for s in (4, 2, 6)]
    return [pair, shifted[1], shifted[2], shifted[0]]


def on_device(
    hidden,
    lengths,
    slot_of,
    kv_cache,
    attn_gain,
    w_query,
    key_matrix,
    value_matrix,
    w_attn_out,
    mamba_gain,
    w_mamba_in,
    w_mamba_dt,
    w_mamba_out,
    conv_weight,
    conv_bias,
    conv_state,
    ssm_state,
    a_log,
    dt_bias,
    skip_gain,
    group_gain,
    mlp_gain,
    w_up,
    w_down,
):
    width = hidden.shape[2]
    slot_row = slot_of.reshape(1, REQ)
    owned = ATTN * 8

    def row(x):
        return x.reshape(1, -1)

    length_row = lengths.reshape(1, REQ)
    kept = (hidden, row(attn_gain), key_matrix, value_matrix, w_query)
    pieces, rows, slot_row, length_row, cache = call(
        qkv_kernel, [(ATTN, STEPS, 2 * 1280 + LANES), (ROWS, width), slot_row, length_row, kv_cache],
        hidden, row(attn_gain), slot_row, length_row, key_matrix, value_matrix, w_query, kv_cache,
        near=True,
        scratch=[pltpu.VMEM(x.shape, x.dtype) for x in kept] + [pltpu.SemaphoreType.DMA((8,))],
        cost=16 * 1024 * 1024,
    )
    pieces = lax.all_to_all(pieces, "attn", 0, 0)
    pieces = call(attend_kernel, [(owned, 512)], pieces, length_row, slot_row, cache)
    pieces = exchange(pieces, "attn", ATTN)
    pieces = call(attn_out_kernel, [(ROWS, width)], pieces, slot_row, w_attn_out)
    pieces = over_tp(pieces)
    pieces, first = call(
        mix_in_kernel, [(ATTN, STEPS, 2 * INNER + 2 * STATES + LANES), (ROWS, width)],
        *pieces, rows, row(mamba_gain), w_mamba_in.reshape(width, -1), w_mamba_dt.T,
    )
    pieces = lax.all_to_all(pieces, "attn", 0, 0)
    pieces = call(
        mamba_kernel, [(owned, 512)],
        pieces, conv_weight, conv_bias, conv_state.reshape(3, 1, -1),
        ssm_state.reshape(INNER, STATES), row(a_log), row(dt_bias), row(skip_gain), group_gain,
    )
    pieces = exchange(pieces, "attn", ATTN)
    pieces = call(project_out_kernel, [(ROWS, width)], pieces, w_mamba_out)
    pieces = over_tp(pieces)
    pieces, second = call(
        up_kernel, [(ATTN, STEPS, INNER + LANES), (ROWS, width)], *pieces, first, row(mlp_gain), w_up
    )
    pieces = lax.all_to_all(pieces, "attn", 0, 0)
    pieces = call(active_kernel, [(owned, 512)], pieces)
    pieces = exchange(pieces, "attn", ATTN)
    pieces = call(project_out_kernel, [(ROWS, width)], pieces, w_down)
    pieces = over_tp(pieces)
    return call(last_kernel, [hidden.shape], *pieces, second)


def solution(mesh):
    in_specs = (
        P(None, None, "attn"),
        P(),
        P(),
        P("attn", None, None, "tp"),
        P("attn"),
        P("attn", "tp"),
        P("attn", "tp"),
        P("attn", "tp"),
        P("tp", "attn"),
        P("attn"),
        P("attn", "tp", None),
        P("attn", "tp"),
        P("tp", "attn"),
        P(None, "tp", None),
        P("tp", None),
        P("attn", None, "tp", None),
        P("attn", "tp", None, None),
        P("tp"),
        P("tp"),
        P("tp"),
        P("tp", None),
        P("attn"),
        P("attn", "tp"),
        P("tp", "attn"),
    )
    out_specs = P(None, None, "attn")
    return jax.shard_map(
        on_device, mesh=mesh, in_specs=in_specs, out_specs=out_specs, check_vma=False
    )
```
